256 devices in a mesh: band: 8 (over x, z_lo), dom: 32 (over z_hi, y, core).
Axes of the slice: x: 4, y: 4, z: 8 (z_hi: 4, z_lo: 2; z = z_hi * 2 + z_lo), core: 2. Of those that a mesh axis runs over, the one named last changes fastest.
Arguments:
- orbitals: float32 [128, 128, 32, 128], P('band', 'dom'), may hold values from -6 to 6
- potential: float32 [128, 32, 128], P('dom'), may hold values from 0 to 1.5
Outputs:
- rotated: float32 [128, 128, 32, 128], P('band', 'dom')
The draws below stay inside these ranges and needn't reach their ends.
All inputs are finite; a program needn't handle non-finite values.
Results may differ from the reference program's by a relative error of at most 0.0043.
Values may be sent and summed in bfloat16 or wider, within the bound.
A program may use at most 128 MiB of HBM per device.

```python
import jax
import jax.numpy as jnp

ORBS = 128
CY = 32
CZ = 128
DEGREE = 6
PASSES = 1
NX = 128


def steps_of(rng, dims, split, least, largest):
    factor_of = 1.0
    for axis_at, shards_of in split:
        heights = jax.random.uniform(jax.random.fold_in(jax.random.fold_in(rng, 6), axis_at), (shards_of,), jnp.float32, least / len(split), largest / len(split))
        factor_of = factor_of * jnp.repeat(jnp.exp(heights), dims[axis_at] // shards_of).reshape((-1,) + (1,) * (len(dims) - 1 - axis_at))
    return factor_of


def scatter_about(own_key, extent, width, reach, pieces=(), held_as=jnp.bfloat16):
    array = jax.random.normal(own_key, extent, jnp.float32) * width
    if len(pieces) > 0:
        array = steps_of(own_key, extent, pieces, -0.22, 0.18) * array
    return jnp.clip(array, min=-reach, max=reach).astype(held_as)


def setup_inputs(seed: int = 0) -> dict:
    streams_of = jax.random.split(jax.random.key(seed), 3)
    orbitals = scatter_about(streams_of[0], (ORBS, NX, CY, CZ), 1.0, 6.0, ((0, 8), (1, 32)), jnp.float32)
    potential = jnp.clip(1.5 * jax.random.uniform(streams_of[1], (NX, CY, CZ), jnp.float32) ** steps_of(streams_of[1], (NX, CY, CZ), ((0, 32),), -0.2, 0.2), 0.0, 1.5)
    return {"orbitals": orbitals, "potential": potential}


centre = 5.5
half = 4.5

def hamiltonian(field, potential):
    lap = -7.5 * field
    for axis in (1, 2, 3):
        lap = lap + 4.0 / 3.0 * (jnp.roll(field, 1, axis) + jnp.roll(field, -1, axis))
        lap = lap - 1.0 / 12.0 * (jnp.roll(field, 2, axis) + jnp.roll(field, -2, axis))
    return potential[None] * field - 0.5 * lap

def filter_pass(block, potential):
    previous = block
    current = (hamiltonian(block, potential) - centre * block) / half
    for step in range(DEGREE - 1):
        following = 2.0 * (hamiltonian(current, potential) - centre * current) / half - previous
        previous, current = (current, following)
    return current

def reference(orbitals, potential):
    filtered = orbitals
    for turn in range(PASSES):
        filtered = filter_pass(filtered, potential)
    flat = filtered.reshape(ORBS, -1).astype(jnp.bfloat16)
    intersection = jnp.dot(flat.astype(jnp.float32), flat.T.astype(jnp.float32), preferred_element_type=jnp.float32) / float(NX * CY * CZ)
    lower = jnp.linalg.cholesky(intersection)
    inverse = jax.scipy.linalg.solve_triangular(lower, jnp.eye(ORBS, dtype=jnp.float32), lower=True)
    inverse_low = inverse.astype(jnp.bfloat16)
    rotated = jnp.dot(inverse_low.astype(jnp.float32), flat.astype(jnp.float32), preferred_element_type=jnp.float32)
    return rotated.reshape(orbitals.shape)
```

```python
import functools

import jax
import jax.numpy as jnp
from jax import lax
from jax.experimental import pallas as pl
from jax.experimental.pallas import tpu as pltpu
from jax.sharding import PartitionSpec as P

MESH = pl.DeviceIdType.MESH
f32, bf16 = jnp.float32, jnp.bfloat16

centre = 5.5
half = 4.5
SCALE = 2.0 / half
DIAGONAL = 0.5 * 7.5 - centre
FIRST = -0.5 * (4.0 / 3.0) * SCALE
SECOND = -1.0 / 16.0

VMEM = pl.BlockSpec(memory_space=pltpu.VMEM)
ANY = pl.BlockSpec(memory_space=pl.ANY)


def remote(src, dst, send_sem, recv_sem, device):
    return pltpu.make_async_remote_copy(
        src_ref=src, dst_ref=dst, send_sem=send_sem, recv_sem=recv_sem, device_id=device, device_id_type=MESH
    )


def wait_bytes(ref, sem):
    pltpu.make_async_copy(ref, ref, sem).wait()


def put(dst, p, o, v):
    dst[p, o, 8:40] = v
    dst[p, o, 0:8] = v[24:32]
    dst[p, o, 40:48] = v[0:8]


def unpack(slot, rec, pot, field):
    for i in range(4):
        pot[4 * slot + i] = (rec[slot, 2, i].astype(f32) + DIAGONAL) * SCALE
        for o in range(2):
            put(field, 4 * slot + i, o, rec[slot, o, i].astype(f32))


def advance(k, first, planes, levels, pot, circulant, sendf):
    src, prev = levels[k - 1], levels[k - 2]
    v = src[pl.ds(first, planes), :, 8:40, :].reshape(planes * 64, 128)
    high = v.astype(bf16)
    low = (v - high.astype(f32)).astype(bf16)
    z = jnp.dot(jnp.concatenate([high, low], axis=1), circulant[...], preferred_element_type=f32)
    for i in range(planes):
        for o in range(2):
            p = first + i
            c = src[p, o, 8:40]
            s1 = src[p - 1, o, 8:40] + src[p + 1, o, 8:40]
            s2 = src[p - 2, o, 8:40] + src[p + 2, o, 8:40]
            s1 = s1 + (src[p, o, 7:39] + src[p, o, 9:41])
            s2 = s2 + (src[p, o, 6:38] + src[p, o, 10:42])
            at = (i * 2 + o) * 32
            w = pot[p] * c + (s1 + z[at : at + 32] + s2 * SECOND) * FIRST
            w = w * 0.5 if k == 1 else w - prev[p, o, 8:40]
            if k < 6:
                put(levels[k], p, o, w)
            else:
                w = w.astype(bf16)
                sendf[2 * (p - 12), o] = w[0:16]
                sendf[2 * (p - 12) + 1, o] = w[16:32]


def filter_kernel(
    orb_hbm, pot_hbm, t_ref, gram_ref,
    orb, potv, send, rec, pot, circulant, sendf, gath, part, r1, q1, r2, q2, r3, q3, *rest
):
    levels, (lsem, ssem, rsem, fsem, gsem, asem) = rest[:6], rest[6:]
    b, d = lax.axis_index("band"), lax.axis_index("dom")
    yc, zh = d % 8, d // 8
    me = yc * 8 + b

    load = pltpu.make_async_copy(orb_hbm, orb, lsem.at[0])
    load.start()
    loadp = pltpu.make_async_copy(pot_hbm, potv, lsem.at[1])
    loadp.start()

    barrier = pltpu.get_barrier_semaphore()

    @pl.loop(1, 64)
    def _(i):
        q = (me + i) % 64
        pl.semaphore_signal(barrier, inc=1, device_id=(q % 8, zh * 8 + q // 8), device_id_type=MESH)

    for i in range(1, 4):
        pl.semaphore_signal(barrier, inc=1, device_id=(b, (zh + i) % 4 * 8 + yc), device_id_type=MESH)

    r = lax.broadcasted_iota(jnp.int32, (128, 128), 0)
    c = lax.broadcasted_iota(jnp.int32, (128, 128), 1)
    apart = (r - c + 128) % 128
    near = jnp.where((apart == 1) | (apart == 127), 1.0, 0.0)
    far = jnp.where((apart == 2) | (apart == 126), SECOND, 0.0)
    for h in range(2):
        circulant[h * 128 : (h + 1) * 128] = (near + far).astype(bf16)

    load.wait()
    loadp.wait()

    @pl.loop(0, 8)
    def _(k):
        for i in range(4):
            for o in range(2):
                send[k, o, i] = orb[2 * k + o, i].astype(bf16)
            send[k, 2, i] = potv[i].astype(bf16)

    rec[3 + yc] = send[yc]
    pl.semaphore_wait(barrier, 66)

    def out_copy(i):
        k = (yc + i) % 8
        return remote(send.at[k], rec.at[3 + yc], ssem.at[i], rsem.at[3 + yc], (b, zh * 8 + k))

    def in_copy(k):
        return remote(send.at[k], rec.at[3 + k], ssem.at[0], rsem.at[3 + k], (b, zh * 8 + k))

    def down(k):
        return remote(rec.at[3 + k], rec.at[11 + k], fsem.at[k], rsem.at[11 + k], (b, (zh + 3) % 4 * 8 + yc))

    def up(k):
        return remote(rec.at[3 + k], rec.at[k - 5], fsem.at[k], rsem.at[k - 5], (b, (zh + 1) % 4 * 8 + yc))

    def forward(k):
        @pl.when(k < 3)
        def _():
            down(k).start()

        @pl.when(k >= 5)
        def _():
            up(k).start()

    for i in range(1, 8):
        out_copy(i).start()
    forward(yc)
    unpack(3 + yc, rec, pot, levels[0])

    @pl.loop(1, 8)
    def _(i):
        k = (yc + 8 - i) % 8
        in_copy(k).wait_recv()
        forward(k)
        unpack(3 + k, rec, pot, levels[0])

    step = functools.partial(advance, levels=levels, pot=pot, circulant=circulant, sendf=sendf)
    for k in range(1, 7):
        planes = (32 - 4 * k) // 2

        @pl.loop(0, 2)
        def _(t):
            step(k, 12 + 2 * k + planes * t, planes)

    for s in range(3):
        up(5 + s).wait_recv()
        down(s).wait_recv()

    @pl.loop(0, 3)
    def _(s):
        unpack(s, rec, pot, levels[0])
        unpack(11 + s, rec, pot, levels[0])

    for k in range(1, 7):

        @pl.loop(0, 2)
        def _(t):
            step(k, 2 * k + t * (44 - 4 * k), 12)

    own = pl.ds(b * 16 + yc * 2, 2)
    gath[own] = sendf[me]

    @pl.loop(1, 64)
    def _(i):
        q = (me + i) % 64
        remote(sendf.at[q], gath.at[own], gsem.at[0], gsem.at[1], (q % 8, zh * 8 + q // 8)).start()

    for i in range(1, 8):
        out_copy(i).wait_send()
    for k in (0, 1, 2):
        down(k).wait_send()
    for k in (5, 6, 7):
        up(k).wait_send()
    wait_bytes(gath.at[0:126], gsem.at[1])

    t = jnp.swapaxes(gath[...].astype(f32), 0, 1).astype(bf16)
    t_ref[...] = t
    x = jnp.concatenate([t[j] for j in range(16)], axis=1)
    gram = lax.dot_general(x, x, (((1,), (1,)), ((), ())), preferred_element_type=f32)
    part[...] = gram.reshape(8, 16, 128)
    r1[yc] = part[yc]
    for i in range(1, 8):
        k = (yc + i) % 8
        remote(part.at[k], r1.at[yc], asem.at[0], asem.at[1], (b, zh * 8 + k)).start()
    wait_bytes(r1.at[0:7], asem.at[1])
    q1[...] = jnp.sum(r1[...], axis=0)
    r2[b] = q1[...]
    for i in range(1, 8):
        remote(q1, r2.at[b], asem.at[2], asem.at[3], ((b + i) % 8, d)).start()
    wait_bytes(r2.at[0:7], asem.at[3])
    q2[...] = jnp.sum(r2[...], axis=0)
    r3[zh] = q2[...]
    for i in range(1, 4):
        remote(q2, r3.at[zh], asem.at[4], asem.at[5], (b, (zh + i) % 4 * 8 + yc)).start()
    wait_bytes(r3.at[0:3], asem.at[5])
    q3[...] = jnp.sum(r3[...], axis=0)
    gram_ref[yc] = q3[...]
    for i in range(1, 8):
        remote(q3, gram_ref.at[yc], asem.at[6], asem.at[7], (b, zh * 8 + (yc + i) % 8)).start()
    wait_bytes(gram_ref.at[0:7], asem.at[7])
    wait_bytes(gath.at[0:126], gsem.at[0])
    wait_bytes(r1.at[0:7], asem.at[0])
    wait_bytes(r2.at[0:7], asem.at[2])
    wait_bytes(r3.at[0:3], asem.at[4])
    wait_bytes(r1.at[0:7], asem.at[6])


def rotate_kernel(w_ref, t_ref, out_ref, sendr, recr, ssem, rsem):
    b, d = lax.axis_index("band"), lax.axis_index("dom")
    barrier = pltpu.get_barrier_semaphore()
    for i in range(1, 8):
        pl.semaphore_signal(barrier, inc=1, device_id=((b + i) % 8, d), device_id_type=MESH)
    for j in range(16):
        rows = jnp.dot(w_ref[...], t_ref[j], preferred_element_type=f32).astype(bf16)
        for k in range(8):
            sendr[k, j] = rows[16 * k : 16 * k + 16]
    recr[b] = sendr[b]
    pl.semaphore_wait(barrier, 7)

    def out_copy(i):
        k = (b + i) % 8
        return remote(sendr.at[k], recr.at[b], ssem.at[i], rsem.at[b], (k, d))

    for i in range(1, 8):
        out_copy(i).start()

    def place(k):
        block = jnp.swapaxes(recr[k].astype(f32), 0, 1)
        out_ref[:, k // 2, pl.ds(pl.multiple_of(k % 2 * 16, 16), 16), :] = block

    place(b)

    @pl.loop(1, 8)
    def _(i):
        k = (b + 8 - i) % 8
        remote(sendr.at[k], recr.at[k], ssem.at[0], rsem.at[k], (k, d)).wait_recv()
        place(k)

    for i in range(1, 8):
        out_copy(i).wait_send()


def body(orbitals, potential):
    dma = pltpu.SemaphoreType.DMA
    t, gram = pl.pallas_call(
        filter_kernel,
        out_shape=(jax.ShapeDtypeStruct((16, 128, 128), bf16), jax.ShapeDtypeStruct((8, 16, 128), f32)),
        in_specs=[ANY, ANY],
        out_specs=(VMEM, VMEM),
        scratch_shapes=[
            pltpu.VMEM((16, 4, 32, 128), f32),
            pltpu.VMEM((4, 32, 128), f32),
            pltpu.VMEM((8, 3, 4, 32, 128), bf16),
            pltpu.VMEM((14, 3, 4, 32, 128), bf16),
            pltpu.VMEM((56, 32, 128), f32),
            pltpu.VMEM((256, 128), bf16),
            pltpu.VMEM((64, 2, 16, 128), bf16),
            pltpu.VMEM((128, 16, 128), bf16),
            pltpu.VMEM((8, 16, 128), f32),
            pltpu.VMEM((8, 16, 128), f32),
            pltpu.VMEM((16, 128), f32),
            pltpu.VMEM((8, 16, 128), f32),
            pltpu.VMEM((16, 128), f32),
            pltpu.VMEM((4, 16, 128), f32),
            pltpu.VMEM((16, 128), f32),
        ]
        + [pltpu.VMEM((56, 2, 48, 128), f32)] * 6
        + [dma((2,)), dma((8,)), dma((14,)), dma((8,)), dma((2,)), dma((8,))],
        compiler_params=pltpu.CompilerParams(collective_id=0, has_side_effects=True, vmem_limit_bytes=52 << 20),
    )(orbitals, potential)
    total_cells = 2048.0 * 256.0
    intersection = gram.reshape(128, 128) / total_cells
    lower = jnp.linalg.cholesky(intersection)
    inverse = jax.scipy.linalg.solve_triangular(lower, jnp.eye(128, dtype=f32), lower=True).astype(bf16)
    return pl.pallas_call(
        rotate_kernel,
        out_shape=jax.ShapeDtypeStruct((16, 4, 32, 128), f32),
        in_specs=[VMEM, VMEM],
        out_specs=VMEM,
        scratch_shapes=[
            pltpu.VMEM((8, 16, 16, 128), bf16),
            pltpu.VMEM((8, 16, 16, 128), bf16),
            dma((8,)),
            dma((8,)),
        ],
        compiler_params=pltpu.CompilerParams(collective_id=1, has_side_effects=True, vmem_limit_bytes=24 << 20),
    )(inverse, t)


def solution(mesh):
    placed = (P("band", "dom", None, None), P("dom", None, None))
    return jax.shard_map(
        body, mesh=mesh, in_specs=placed, out_specs=P("band", "dom", None, None), check_vma=False
    )
```

```python
import functools

import jax
import jax.numpy as jnp
from jax import lax
from jax.experimental import pallas as pl
from jax.experimental.pallas import tpu as pltpu
from jax.sharding import PartitionSpec as P

MESH = pl.DeviceIdType.MESH
f32, bf16 = jnp.float32, jnp.bfloat16

centre = 5.5
half = 4.5
SCALE = 2.0 / half
DIAGONAL = 0.5 * 7.5 - centre
FIRST = -0.5 * (4.0 / 3.0) * SCALE
SECOND = -1.0 / 16.0

VMEM = pl.BlockSpec(memory_space=pltpu.VMEM)
ANY = pl.BlockSpec(memory_space=pl.ANY)


def remote(src, dst, send_sem, recv_sem, device):
    return pltpu.make_async_remote_copy(
        src_ref=src, dst_ref=dst, send_sem=send_sem, recv_sem=recv_sem, device_id=device, device_id_type=MESH
    )


def wait_bytes(ref, sem):
    pltpu.make_async_copy(ref, ref, sem).wait()


def put(dst, p, o, v):
    dst[p, o, 8:40] = v
    dst[p, o, 0:8] = v[24:32]
    dst[p, o, 40:48] = v[0:8]


def unpack(slot, rec, pot, field):
    for i in range(4):
        pot[4 * slot + i] = (rec[slot, 2, i].astype(f32) + DIAGONAL) * SCALE
        for o in range(2):
            put(field, 4 * slot + i, o, rec[slot, o, i].astype(f32))


def advance(k, first, planes, levels, pot, circulant, sendf):
    src, prev = levels[k - 1], levels[k - 2]
    v = src[pl.ds(first, planes), :, 8:40, :].reshape(planes * 64, 128)
    high = v.astype(bf16)
    low = (v - high.astype(f32)).astype(bf16)
    z = jnp.dot(jnp.concatenate([high, low], axis=1), circulant[...], preferred_element_type=f32)
    for i in range(planes):
        for o in range(2):
            p = first + i
            c = src[p, o, 8:40]
            s1 = src[p - 1, o, 8:40] + src[p + 1, o, 8:40]
            s2 = src[p - 2, o, 8:40] + src[p + 2, o, 8:40]
            s1 = s1 + (src[p, o, 7:39] + src[p, o, 9:41])
            s2 = s2 + (src[p, o, 6:38] + src[p, o, 10:42])
            at = (i * 2 + o) * 32
            w = pot[p] * c + (s1 + z[at : at + 32] + s2 * SECOND) * FIRST
            w = w * 0.5 if k == 1 else w - prev[p, o, 8:40]
            if k < 6:
                put(levels[k], p, o, w)
            else:
                w = w.astype(bf16)
                sendf[2 * (p - 12), o] = w[0:16]
                sendf[2 * (p - 12) + 1, o] = w[16:32]


def inverse_factor(m):
    n, nb = 128, 16
    row = lax.broadcasted_iota(jnp.int32, (nb, n), 0)
    lane = lax.broadcasted_iota(jnp.int32, (nb, n), 1)
    out = []
    for k in range(n // nb):
        at, lo = k * nb, (k + 1) * nb
        x = m[at:lo]
        cols = [jnp.broadcast_to(x[:, at + t : at + t + 1], (nb, n)) for t in range(nb)]
        own = (lane >= at) & (lane < lo)
        x = jnp.where(own, jnp.where(lane - at == row, 1.0, 0.0), x)
        w = jnp.zeros_like(x)
        for t in range(nb):
            here = row == t
            pivot = jnp.broadcast_to(cols[t][t : t + 1], (nb, n))
            inv = 1.0 / pivot
            r = jnp.broadcast_to(x[t : t + 1], (nb, n))
            w = jnp.where(here, r * lax.rsqrt(pivot), w)
            mult = jnp.where(here, 1.0 - inv, cols[t] * inv)
            x = x - mult * r
            for u in range(t + 1, nb):
                cols[u] = cols[u] - mult * jnp.broadcast_to(cols[u][t : t + 1], (nb, n))
        out.append(jnp.where(lane < lo, w, 0.0))
        if lo < n:
            below = m[lo:]
            lane_b = lax.broadcasted_iota(jnp.int32, below.shape, 1)
            padded = [jnp.zeros((at, n), f32)] * (at > 0) + [x, jnp.zeros((n - lo, n), f32)]
            change = jnp.dot(
                below, jnp.concatenate(padded, 0), precision=lax.Precision.HIGHEST, preferred_element_type=f32
            )
            kept = jnp.where((lane_b >= at) & (lane_b < lo), 0.0, below)
            m = jnp.concatenate([m[:lo], kept - change], axis=0)
    return out


def kernel(
    orb_hbm, pot_hbm, out_hbm,
    orb, potv, send, rec, pot, circulant, sendf, gath, part, r1, q1, r2, q2, r3, q3, gram_ref, t_ref, sendr, recr, outv, *rest
):
    levels, (lsem, ssem, rsem, fsem, gsem, asem, bsem, csem, osem) = rest[:6], rest[6:]
    b, d = lax.axis_index("band"), lax.axis_index("dom")
    yc, zh = d % 8, d // 8
    me = yc * 8 + b

    load = pltpu.make_async_copy(orb_hbm, orb, lsem.at[0])
    load.start()
    loadp = pltpu.make_async_copy(pot_hbm, potv, lsem.at[1])
    loadp.start()

    barrier = pltpu.get_barrier_semaphore()

    @pl.loop(1, 64)
    def _(i):
        q = (me + i) % 64
        pl.semaphore_signal(barrier, inc=1, device_id=(q % 8, zh * 8 + q // 8), device_id_type=MESH)

    for i in range(1, 4):
        pl.semaphore_signal(barrier, inc=1, device_id=(b, (zh + i) % 4 * 8 + yc), device_id_type=MESH)

    r = lax.broadcasted_iota(jnp.int32, (128, 128), 0)
    c = lax.broadcasted_iota(jnp.int32, (128, 128), 1)
    apart = (r - c + 128) % 128
    near = jnp.where((apart == 1) | (apart == 127), 1.0, 0.0)
    far = jnp.where((apart == 2) | (apart == 126), SECOND, 0.0)
    for h in range(2):
        circulant[h * 128 : (h + 1) * 128] = (near + far).astype(bf16)

    load.wait()
    loadp.wait()

    @pl.loop(0, 8)
    def _(k):
        for i in range(4):
            for o in range(2):
                send[k, o, i] = orb[2 * k + o, i].astype(bf16)
            send[k, 2, i] = potv[i].astype(bf16)

    rec[3 + yc] = send[yc]
    pl.semaphore_wait(barrier, 66)

    def out_copy(i):
        k = (yc + i) % 8
        return remote(send.at[k], rec.at[3 + yc], ssem.at[i], rsem.at[3 + yc], (b, zh * 8 + k))

    def in_copy(k):
        return remote(send.at[k], rec.at[3 + k], ssem.at[0], rsem.at[3 + k], (b, zh * 8 + k))

    def down(k):
        return remote(rec.at[3 + k], rec.at[11 + k], fsem.at[k], rsem.at[11 + k], (b, (zh + 3) % 4 * 8 + yc))

    def up(k):
        return remote(rec.at[3 + k], rec.at[k - 5], fsem.at[k], rsem.at[k - 5], (b, (zh + 1) % 4 * 8 + yc))

    def forward(k):
        @pl.when(k < 3)
        def _():
            down(k).start()

        @pl.when(k >= 5)
        def _():
            up(k).start()

    for i in range(1, 8):
        out_copy(i).start()
    forward(yc)
    unpack(3 + yc, rec, pot, levels[0])

    @pl.loop(1, 8)
    def _(i):
        k = (yc + 8 - i) % 8
        in_copy(k).wait_recv()
        forward(k)
        unpack(3 + k, rec, pot, levels[0])

    step = functools.partial(advance, levels=levels, pot=pot, circulant=circulant, sendf=sendf)
    for k in range(1, 7):
        planes = (32 - 4 * k) // 2

        @pl.loop(0, 2)
        def _(t):
            step(k, 12 + 2 * k + planes * t, planes)

    for s in range(3):
        up(5 + s).wait_recv()
        down(s).wait_recv()

    @pl.loop(0, 3)
    def _(s):
        unpack(s, rec, pot, levels[0])
        unpack(11 + s, rec, pot, levels[0])

    for k in range(1, 7):

        @pl.loop(0, 2)
        def _(t):
            step(k, 2 * k + t * (44 - 4 * k), 12)

    own = pl.ds(b * 16 + yc * 2, 2)
    gath[own] = sendf[me]

    @pl.loop(1, 64)
    def _(i):
        q = (me + i) % 64
        remote(sendf.at[q], gath.at[own], gsem.at[0], gsem.at[1], (q % 8, zh * 8 + q // 8)).start()

    for i in range(1, 8):
        out_copy(i).wait_send()
    for k in (0, 1, 2):
        down(k).wait_send()
    for k in (5, 6, 7):
        up(k).wait_send()
    wait_bytes(gath.at[0:126], gsem.at[1])

    t = jnp.swapaxes(gath[...].astype(f32), 0, 1).astype(bf16)
    t_ref[...] = t
    x = jnp.concatenate([t[j] for j in range(16)], axis=1)
    gram = lax.dot_general(x, x, (((1,), (1,)), ((), ())), preferred_element_type=f32)
    part[...] = gram.reshape(8, 16, 128)
    r1[yc] = part[yc]
    for i in range(1, 8):
        k = (yc + i) % 8
        remote(part.at[k], r1.at[yc], asem.at[0], asem.at[1], (b, zh * 8 + k)).start()
    wait_bytes(r1.at[0:7], asem.at[1])
    q1[...] = jnp.sum(r1[...], axis=0)
    r2[b] = q1[...]
    for i in range(1, 8):
        remote(q1, r2.at[b], asem.at[2], asem.at[3], ((b + i) % 8, d)).start()
    wait_bytes(r2.at[0:7], asem.at[3])
    q2[...] = jnp.sum(r2[...], axis=0)
    r3[zh] = q2[...]
    for i in range(1, 4):
        remote(q2, r3.at[zh], asem.at[4], asem.at[5], (b, (zh + i) % 4 * 8 + yc)).start()
    wait_bytes(r3.at[0:3], asem.at[5])
    q3[...] = jnp.sum(r3[...], axis=0)
    gram_ref[yc] = q3[...]
    for i in range(1, 8):
        remote(q3, gram_ref.at[yc], asem.at[6], asem.at[7], (b, zh * 8 + (yc + i) % 8)).start()
    wait_bytes(gram_ref.at[0:7], asem.at[7])

    inverse = inverse_factor(gram_ref[...].reshape(128, 128) * (1.0 / 2.0**19))
    w = jnp.concatenate([block.astype(bf16) for block in inverse], axis=0)
    for j in range(16):
        rows = jnp.dot(w, t_ref[j], preferred_element_type=f32).astype(bf16)
        for k in range(8):
            sendr[k, j] = rows[16 * k : 16 * k + 16]

    def back_copy(i):
        k = (b + i) % 8
        return remote(sendr.at[k], recr.at[b], bsem.at[i], csem.at[b], (k, d))

    def place_copy(k):
        rows = pl.ds(pl.multiple_of(k % 2 * 16, 16), 16)
        return pltpu.make_async_copy(outv.at[k], out_hbm.at[:, k // 2, rows, :], osem.at[k])

    def place(k):
        outv[k] = jnp.swapaxes(recr[k].astype(f32), 0, 1)
        place_copy(k).start()

    for i in range(1, 8):
        back_copy(i).start()
    recr[b] = sendr[b]
    place(b)

    @pl.loop(1, 8)
    def _(i):
        k = (b + 8 - i) % 8
        remote(sendr.at[k], recr.at[k], bsem.at[0], csem.at[k], (k, d)).wait_recv()
        place(k)

    wait_bytes(gath.at[0:126], gsem.at[0])
    wait_bytes(r1.at[0:7], asem.at[0])
    wait_bytes(r2.at[0:7], asem.at[2])
    wait_bytes(r3.at[0:3], asem.at[4])
    wait_bytes(r1.at[0:7], asem.at[6])
    for i in range(1, 8):
        back_copy(i).wait_send()

    @pl.loop(0, 8)
    def _(k):
        place_copy(k).wait()


def body(orbitals, potential):
    dma = pltpu.SemaphoreType.DMA
    return pl.pallas_call(
        kernel,
        out_shape=jax.ShapeDtypeStruct((16, 4, 32, 128), f32),
        in_specs=[ANY, ANY],
        out_specs=ANY,
        scratch_shapes=[
            pltpu.VMEM((16, 4, 32, 128), f32),
            pltpu.VMEM((4, 32, 128), f32),
            pltpu.VMEM((8, 3, 4, 32, 128), bf16),
            pltpu.VMEM((14, 3, 4, 32, 128), bf16),
            pltpu.VMEM((56, 32, 128), f32),
            pltpu.VMEM((256, 128), bf16),
            pltpu.VMEM((64, 2, 16, 128), bf16),
            pltpu.VMEM((128, 16, 128), bf16),
            pltpu.VMEM((8, 16, 128), f32),
            pltpu.VMEM((8, 16, 128), f32),
            pltpu.VMEM((16, 128), f32),
            pltpu.VMEM((8, 16, 128), f32),
            pltpu.VMEM((16, 128), f32),
            pltpu.VMEM((4, 16, 128), f32),
            pltpu.VMEM((16, 128), f32),
            pltpu.VMEM((8, 16, 128), f32),
            pltpu.VMEM((16, 128, 128), bf16),
            pltpu.VMEM((8, 16, 16, 128), bf16),
            pltpu.VMEM((8, 16, 16, 128), bf16),
            pltpu.VMEM((8, 16, 16, 128), f32),
        ]
        + [pltpu.VMEM((56, 2, 48, 128), f32)] * 6
        + [dma((2,)), dma((8,)), dma((14,)), dma((8,)), dma((2,)), dma((8,)), dma((8,)), dma((8,)), dma((8,))],
        compiler_params=pltpu.CompilerParams(collective_id=0, has_side_effects=True, vmem_limit_bytes=60 << 20),
    )(orbitals, potential)


def solution(mesh):
    placed = (P("band", "dom", None, None), P("dom", None, None))
    return jax.shard_map(
        body, mesh=mesh, in_specs=placed, out_specs=P("band", "dom", None, None), check_vma=False
    )
```

```python
import functools

import jax
import jax.numpy as jnp
from jax import lax
from jax.experimental import pallas as pl
from jax.experimental.pallas import tpu as pltpu
from jax.sharding import PartitionSpec as P

MESH = pl.DeviceIdType.MESH
f32, bf16 = jnp.float32, jnp.bfloat16

centre = 5.5
half = 4.5
SCALE = 2.0 / half
DIAGONAL = 0.5 * 7.5 - centre
FIRST = -0.5 * (4.0 / 3.0) * SCALE
SECOND = -1.0 / 16.0

VMEM = pl.BlockSpec(memory_space=pltpu.VMEM)
ANY = pl.BlockSpec(memory_space=pl.ANY)


def remote(src, dst, send_sem, recv_sem, device):
    return pltpu.make_async_remote_copy(
        src_ref=src, dst_ref=dst, send_sem=send_sem, recv_sem=recv_sem, device_id=device, device_id_type=MESH
    )


def wait_bytes(ref, sem):
    pltpu.make_async_copy(ref, ref, sem).wait()


def put(dst, p, o, v):
    dst[p, o, 8:40] = v
    dst[p, o, 0:8] = v[24:32]
    dst[p, o, 40:48] = v[0:8]


def unpack(slot, rec, field):
    for i in range(4):
        for o in range(2):
            put(field, 4 * slot + i, o, rec[slot, o, i].astype(f32))


def scaled(plane):
    return (plane.astype(f32) + DIAGONAL) * SCALE


def advance(k, segments, levels, pot, circulant, sendf):
    src, prev = levels[k - 1], levels[k - 2]
    for first, planes in segments:
        v = src[pl.ds(first, planes), :, 8:40, :].reshape(planes * 64, 128)
        high = v.astype(bf16)
        low = (v - high.astype(f32)).astype(bf16)
        z = jnp.dot(jnp.concatenate([high, low], axis=1), circulant[...], preferred_element_type=f32)
        for i in range(planes):
            for o in range(2):
                p = first + i
                c = src[p, o, 8:40]
                s1 = src[p - 1, o, 8:40] + src[p + 1, o, 8:40]
                s2 = src[p - 2, o, 8:40] + src[p + 2, o, 8:40]
                s1 = s1 + (src[p, o, 7:39] + src[p, o, 9:41])
                s2 = s2 + (src[p, o, 6:38] + src[p, o, 10:42])
                at = (i * 2 + o) * 32
                w = pot[p] * c + (s1 + z[at : at + 32] + s2 * SECOND) * FIRST
                w = w * 0.5 if k == 1 else w - prev[p, o, 8:40]
                if k < 6:
                    put(levels[k], p, o, w)
                else:
                    w = w.astype(bf16)
                    sendf[2 * (p - 12), o] = w[0:16]
                    sendf[2 * (p - 12) + 1, o] = w[16:32]


def inverse_factor(m):
    n, nb = 128, 16
    row = lax.broadcasted_iota(jnp.int32, (nb, n), 0)
    lane = lax.broadcasted_iota(jnp.int32, (nb, n), 1)
    out = []
    for k in range(n // nb):
        at, lo = k * nb, (k + 1) * nb
        x = m[at:lo]
        cols = [jnp.broadcast_to(x[:, at + t : at + t + 1], (nb, n)) for t in range(nb)]
        own = (lane >= at) & (lane < lo)
        x = jnp.where(own, jnp.where(lane - at == row, 1.0, 0.0), x)
        w = jnp.zeros_like(x)
        for t in range(nb):
            here = row == t
            pivot = jnp.broadcast_to(cols[t][t : t + 1], (nb, n))
            inv = 1.0 / pivot
            r = jnp.broadcast_to(x[t : t + 1], (nb, n))
            w = jnp.where(here, r * lax.rsqrt(pivot), w)
            mult = jnp.where(here, 1.0 - inv, cols[t] * inv)
            x = x - mult * r
            for u in range(t + 1, nb):
                cols[u] = cols[u] - mult * jnp.broadcast_to(cols[u][t : t + 1], (nb, n))
        out.append(jnp.where(lane < lo, w, 0.0))
        if lo < n:
            below = m[lo:]
            lane_b = lax.broadcasted_iota(jnp.int32, below.shape, 1)
            padded = [jnp.zeros((at, n), f32)] * (at > 0) + [x, jnp.zeros((n - lo, n), f32)]
            change = jnp.dot(
                below, jnp.concatenate(padded, 0), precision=lax.Precision.HIGHEST, preferred_element_type=f32
            )
            kept = jnp.where((lane_b >= at) & (lane_b < lo), 0.0, below)
            m = jnp.concatenate([m[:lo], kept - change], axis=0)
    return out


def kernel(
    orb_hbm, pot_hbm, out_hbm,
    orb, potv, potb, potp, poth, potg, poti, send, rec, pot, circulant, sendf, gath,
    part, r1, q1, r2, q2, r3, q3, gram_ref, t_ref, sendr, recr, outv, *rest
):
    levels, (lsem, psem, ssem, rsem, fsem, gsem, asem, bsem, csem, osem) = rest[:6], rest[6:]
    b, d = lax.axis_index("band"), lax.axis_index("dom")
    yc, zh = d % 8, d // 8
    x, lower = b // 2, b % 2
    me = yc * 8 + b
    above, below = (zh + 1) % 4 * 8, (zh + 3) % 4 * 8

    loadp = pltpu.make_async_copy(pot_hbm, potv, lsem.at[1])
    loadp.start()
    load = pltpu.make_async_copy(orb_hbm, orb, lsem.at[0])
    load.start()

    barrier = pltpu.get_barrier_semaphore()

    def greet(device):
        pl.semaphore_signal(barrier, inc=1, device_id=device, device_id_type=MESH)

    @pl.loop(1, 64)
    def _(i):
        q = (me + i) % 64
        greet((q % 8, zh * 8 + q // 8))

    @pl.loop(0, 8)
    def _(k):
        greet((b, above + k))
        greet((b, below + k))

    greet((b, (zh + 2) % 4 * 8 + yc))

    r = lax.broadcasted_iota(jnp.int32, (128, 128), 0)
    c = lax.broadcasted_iota(jnp.int32, (128, 128), 1)
    apart = (r - c + 128) % 128
    near = jnp.where((apart == 1) | (apart == 127), 1.0, 0.0)
    far = jnp.where((apart == 2) | (apart == 126), SECOND, 0.0)
    for h in range(2):
        circulant[h * 128 : (h + 1) * 128] = (near + far).astype(bf16)

    loadp.wait()
    potb[...] = potv[...].astype(bf16)
    potp[yc] = potb[x]
    pl.semaphore_wait(barrier, 80)

    for i in range(1, 8):
        remote(potb.at[x], potp.at[yc], psem.at[0], psem.at[1], (b, zh * 8 + (yc + i) % 8)).start()

    @pl.when(yc < 3)
    def _():
        for k in range(8):
            remote(potb.at[x], poth.at[3 + yc], psem.at[2], psem.at[3], (b, below + k)).start()

    @pl.when(yc >= 5)
    def _():
        for k in range(8):
            remote(potb.at[x], poth.at[yc - 5], psem.at[2], psem.at[3], (b, above + k)).start()

    load.wait()

    def out_copy(k):
        return remote(send.at[k], rec.at[3 + yc], ssem.at[k], rsem.at[3 + yc], (b, zh * 8 + k))

    def in_copy(k):
        return remote(send.at[k], rec.at[3 + k], ssem.at[0], rsem.at[3 + k], (b, zh * 8 + k))

    def down(k):
        return remote(rec.at[3 + k], rec.at[11 + k], fsem.at[k], rsem.at[11 + k], (b, below + yc))

    def up(k):
        return remote(rec.at[3 + k], rec.at[k - 5], fsem.at[k], rsem.at[k - 5], (b, above + yc))

    def along_x(i, src, dst, sem):
        return remote(src, dst, psem.at[sem], psem.at[sem + 1], ((x + i) % 4 * 2 + lower, d))

    @pl.loop(1, 8)
    def _(i):
        k = (yc + i) % 8
        for j in range(4):
            for o in range(2):
                send[k, o, j] = orb[2 * k + o, j].astype(bf16)
        out_copy(k).start()

    for j in range(4):
        for o in range(2):
            rec[3 + yc, o, j] = orb[2 * yc + o, j].astype(bf16)

    wait_bytes(potp.at[0:7], psem.at[1])
    for i in range(1, 4):
        along_x(i, potp, potg.at[x], 4).start()
    potg[x] = potp[...]
    wait_bytes(poth, psem.at[3])
    for i in range(1, 4):
        along_x(i, poth, poti.at[x], 6).start()
    poti[x] = poth[...]

    for k in (0, 7, 1, 6, 2, 5, 3, 4):

        @pl.when(yc != k)
        def _():
            in_copy(k).wait_recv()

        if k < 3:
            down(k).start()
        if k >= 5:
            up(k).start()
        unpack(3 + k, rec, levels[0])

    wait_bytes(potg.at[0:3], psem.at[5])

    @pl.loop(0, 8)
    def _(s):
        for i in range(4):
            pot[12 + 4 * s + i] = scaled(potg[i, s])

    step = functools.partial(advance, levels=levels, pot=pot, circulant=circulant, sendf=sendf)
    for k in range(1, 7):
        planes = (32 - 4 * k) // 2

        @pl.loop(0, 2)
        def _(t):
            step(k, [(12 + 2 * k + planes * t, planes)])

    own = pl.ds(b * 16 + yc * 2, 2)

    def deliver(to):
        @pl.loop(0, 8)
        def _(i):
            band = (b + i) % 8
            q = to * 8 + band

            @pl.when(q != me)
            def _():
                remote(sendf.at[q], gath.at[own], gsem.at[0], gsem.at[1], (band, zh * 8 + to)).start()

    deliver(3)
    deliver(4)

    wait_bytes(poti.at[0:3], psem.at[7])
    for s in range(3):
        for i in range(4):
            pot[4 * s + i] = scaled(poti[i, s])
            pot[44 + 4 * s + i] = scaled(poti[i, 3 + s])

    @pl.loop(0, 3)
    def _(s):
        up(7 - s).wait_recv()
        down(s).wait_recv()
        unpack(2 - s, rec, levels[0])
        unpack(11 + s, rec, levels[0])
        for k in range(1, 7):
            step(k, [(8 - 4 * s + 2 * k, 4), (44 + 4 * s - 2 * k, 4)])
        deliver(2 - s)
        deliver(5 + s)

    gath[own] = sendf[me]

    wait_bytes(potp.at[0:7], psem.at[0])

    @pl.when((yc < 3) | (yc >= 5))
    def _():
        wait_bytes(potp, psem.at[2])

    wait_bytes(potg.at[0:3], psem.at[4])
    wait_bytes(poti.at[0:3], psem.at[6])
    for i in range(1, 8):
        out_copy((yc + i) % 8).wait_send()
    for k in (0, 1, 2):
        down(k).wait_send()
    for k in (5, 6, 7):
        up(k).wait_send()
    wait_bytes(gath.at[0:126], gsem.at[1])

    t = jnp.swapaxes(gath[...].astype(f32), 0, 1).astype(bf16)
    t_ref[...] = t
    x = jnp.concatenate([t[j] for j in range(16)], axis=1)
    gram = lax.dot_general(x, x, (((1,), (1,)), ((), ())), preferred_element_type=f32)
    part[...] = gram.reshape(8, 16, 128)
    r1[yc] = part[yc]
    for i in range(1, 8):
        k = (yc + i) % 8
        remote(part.at[k], r1.at[yc], asem.at[0], asem.at[1], (b, zh * 8 + k)).start()
    wait_bytes(r1.at[0:7], asem.at[1])
    q1[...] = jnp.sum(r1[...], axis=0)
    r2[b] = q1[...]
    for i in range(1, 8):
        remote(q1, r2.at[b], asem.at[2], asem.at[3], ((b + i) % 8, d)).start()
    wait_bytes(r2.at[0:7], asem.at[3])
    q2[...] = jnp.sum(r2[...], axis=0)
    r3[zh] = q2[...]
    for i in range(1, 4):
        remote(q2, r3.at[zh], asem.at[4], asem.at[5], (b, (zh + i) % 4 * 8 + yc)).start()
    wait_bytes(r3.at[0:3], asem.at[5])
    q3[...] = jnp.sum(r3[...], axis=0)
    gram_ref[yc] = q3[...]
    for i in range(1, 8):
        remote(q3, gram_ref.at[yc], asem.at[6], asem.at[7], (b, zh * 8 + (yc + i) % 8)).start()
    wait_bytes(gram_ref.at[0:7], asem.at[7])

    inverse = inverse_factor(gram_ref[...].reshape(128, 128) * (1.0 / 2.0**19))
    w = jnp.concatenate([block.astype(bf16) for block in inverse], axis=0)
    for j in range(16):
        rows = jnp.dot(w, t_ref[j], preferred_element_type=f32).astype(bf16)
        for k in range(8):
            sendr[k, j] = rows[16 * k : 16 * k + 16]

    def back_copy(i):
        k = (b + i) % 8
        return remote(sendr.at[k], recr.at[b], bsem.at[i], csem.at[b], (k, d))

    def place_copy(k):
        rows = pl.ds(pl.multiple_of(k % 2 * 16, 16), 16)
        return pltpu.make_async_copy(outv.at[k], out_hbm.at[:, k // 2, rows, :], osem.at[k])

    def place(k):
        outv[k] = jnp.swapaxes(recr[k].astype(f32), 0, 1)
        place_copy(k).start()

    for i in range(1, 8):
        back_copy(i).start()
    recr[b] = sendr[b]
    place(b)

    @pl.loop(1, 8)
    def _(i):
        k = (b + 8 - i) % 8
        remote(sendr.at[k], recr.at[k], bsem.at[0], csem.at[k], (k, d)).wait_recv()
        place(k)

    wait_bytes(gath.at[0:126], gsem.at[0])
    wait_bytes(r1.at[0:7], asem.at[0])
    wait_bytes(r2.at[0:7], asem.at[2])
    wait_bytes(r3.at[0:3], asem.at[4])
    wait_bytes(r1.at[0:7], asem.at[6])
    for i in range(1, 8):
        back_copy(i).wait_send()

    @pl.loop(0, 8)
    def _(k):
        place_copy(k).wait()


def body(orbitals, potential):
    dma = pltpu.SemaphoreType.DMA
    return pl.pallas_call(
        kernel,
        out_shape=jax.ShapeDtypeStruct((16, 4, 32, 128), f32),
        in_specs=[ANY, ANY],
        out_specs=ANY,
        scratch_shapes=[
            pltpu.VMEM((16, 4, 32, 128), f32),
            pltpu.VMEM((4, 32, 128), f32),
            pltpu.VMEM((4, 32, 128), bf16),
            pltpu.VMEM((8, 32, 128), bf16),
            pltpu.VMEM((6, 32, 128), bf16),
            pltpu.VMEM((4, 8, 32, 128), bf16),
            pltpu.VMEM((4, 6, 32, 128), bf16),
            pltpu.VMEM((8, 2, 4, 32, 128), bf16),
            pltpu.VMEM((14, 2, 4, 32, 128), bf16),
            pltpu.VMEM((56, 32, 128), f32),
            pltpu.VMEM((256, 128), bf16),
            pltpu.VMEM((64, 2, 16, 128), bf16),
            pltpu.VMEM((128, 16, 128), bf16),
            pltpu.VMEM((8, 16, 128), f32),
            pltpu.VMEM((8, 16, 128), f32),
            pltpu.VMEM((16, 128), f32),
            pltpu.VMEM((8, 16, 128), f32),
            pltpu.VMEM((16, 128), f32),
            pltpu.VMEM((4, 16, 128), f32),
            pltpu.VMEM((16, 128), f32),
            pltpu.VMEM((8, 16, 128), f32),
            pltpu.VMEM((16, 128, 128), bf16),
            pltpu.VMEM((8, 16, 16, 128), bf16),
            pltpu.VMEM((8, 16, 16, 128), bf16),
            pltpu.VMEM((8, 16, 16, 128), f32),
        ]
        + [pltpu.VMEM((56, 2, 48, 128), f32)] * 6
        + [dma((2,)), dma((8,)), dma((8,)), dma((14,)), dma((8,)), dma((2,)), dma((8,)), dma((8,)), dma((8,)), dma((8,))],
        compiler_params=pltpu.CompilerParams(collective_id=0, has_side_effects=True, vmem_limit_bytes=60 << 20),
    )(orbitals, potential)


def solution(mesh):
    placed = (P("band", "dom", None, None), P("dom", None, None))
    return jax.shard_map(
        body, mesh=mesh, in_specs=placed, out_specs=P("band", "dom", None, None), check_vma=False
    )
```

```python
import functools

import jax
import jax.numpy as jnp
from jax import lax
from jax.experimental import pallas as pl
from jax.experimental.pallas import tpu as pltpu
from jax.sharding import PartitionSpec as P

MESH = pl.DeviceIdType.MESH
f32, bf16 = jnp.float32, jnp.bfloat16

centre = 5.5
half = 4.5
SCALE = 2.0 / half
DIAGONAL = 0.5 * 7.5 - centre
FIRST = -0.5 * (4.0 / 3.0) * SCALE
SECOND = -1.0 / 16.0

VMEM = pl.BlockSpec(memory_space=pltpu.VMEM)
ANY = pl.BlockSpec(memory_space=pl.ANY)


def remote(src, dst, send_sem, recv_sem, device):
    return pltpu.make_async_remote_copy(
        src_ref=src, dst_ref=dst, send_sem=send_sem, recv_sem=recv_sem, device_id=device, device_id_type=MESH
    )


def wait_bytes(ref, sem):
    pltpu.make_async_copy(ref, ref, sem).wait()


def put(dst, p, o, v):
    dst[p, o, 8:40] = v
    dst[p, o, 0:8] = v[24:32]
    dst[p, o, 40:48] = v[0:8]


def unpack(slot, o, rec, field):
    for i in range(4):
        put(field, 4 * slot + i, o, rec[o, slot, i].astype(f32))


def scaled(plane):
    return (plane.astype(f32) + DIAGONAL) * SCALE


def advance(k, o, segments, levels, pot, circulant, sendf):
    src, prev = levels[k - 1], levels[k - 2]
    for first, planes in segments:
        window = [src[first - 2 + j, o, 8:40] for j in range(planes + 4)]
        v = jnp.concatenate(window[2:-2], axis=0)
        high = v.astype(bf16)
        low = (v - high.astype(f32)).astype(bf16)
        z = jnp.dot(jnp.concatenate([high, low], axis=1), circulant[...], preferred_element_type=f32)
        for i in range(planes):
            p = first + i
            s1 = window[i + 1] + window[i + 3]
            s2 = window[i] + window[i + 4]
            s1 = s1 + (src[p, o, 7:39] + src[p, o, 9:41])
            s2 = s2 + (src[p, o, 6:38] + src[p, o, 10:42])
            w = pot[p] * window[i + 2] + (s1 + z[32 * i : 32 * i + 32] + s2 * SECOND) * FIRST
            w = w * 0.5 if k == 1 else w - prev[p, o, 8:40]
            if k < 6:
                put(levels[k], p, o, w)
            else:
                w = w.astype(bf16)
                sendf[2 * (p - 12), o] = w[0:16]
                sendf[2 * (p - 12) + 1, o] = w[16:32]


def inverse_factor(m):
    n, nb = 128, 16
    row = lax.broadcasted_iota(jnp.int32, (nb, n), 0)
    lane = lax.broadcasted_iota(jnp.int32, (nb, n), 1)
    out = []
    for k in range(n // nb):
        at, lo = k * nb, (k + 1) * nb
        x = m[at:lo]
        cols = [jnp.broadcast_to(x[:, at + t : at + t + 1], (nb, n)) for t in range(nb)]
        own = (lane >= at) & (lane < lo)
        x = jnp.where(own, jnp.where(lane - at == row, 1.0, 0.0), x)
        w = jnp.zeros_like(x)
        for t in range(nb):
            here = row == t
            pivot = jnp.broadcast_to(cols[t][t : t + 1], (nb, n))
            inv = 1.0 / pivot
            r = jnp.broadcast_to(x[t : t + 1], (nb, n))
            w = jnp.where(here, r * lax.rsqrt(pivot), w)
            mult = jnp.where(here, 1.0 - inv, cols[t] * inv)
            x = x - mult * r
            for u in range(t + 1, nb):
                cols[u] = cols[u] - mult * jnp.broadcast_to(cols[u][t : t + 1], (nb, n))
        out.append(jnp.where(lane < lo, w, 0.0))
        if lo < n:
            below = m[lo:]
            lane_b = lax.broadcasted_iota(jnp.int32, below.shape, 1)
            padded = [jnp.zeros((at, n), f32)] * (at > 0) + [x, jnp.zeros((n - lo, n), f32)]
            change = jnp.dot(
                below, jnp.concatenate(padded, 0), precision=lax.Precision.HIGHEST, preferred_element_type=f32
            )
            kept = jnp.where((lane_b >= at) & (lane_b < lo), 0.0, below)
            m = jnp.concatenate([m[:lo], kept - change], axis=0)
    return out


def kernel(
    orb_hbm, pot_hbm, out_hbm,
    orb, potv, potb, potp, poth, potg, poti, send, rec, pot, circulant, sendf, gath,
    part, r1, q1, r2, q2, gram_ref, t_ref, rot, sendr, *rest
):
    levels, (lsem, psem, ssem, rsem, fsem, gsem, asem, bsem, csem, osem) = rest[:6], rest[6:]
    b, d = lax.axis_index("band"), lax.axis_index("dom")
    yc, zh = d % 8, d // 8
    x, lower = b // 2, b % 2
    me = yc * 8 + b
    above, below = (zh + 1) % 4 * 8, (zh + 3) % 4 * 8

    loadp = pltpu.make_async_copy(pot_hbm, potv, lsem.at[1])
    loadp.start()
    load = pltpu.make_async_copy(orb_hbm, orb, lsem.at[0])
    load.start()

    barrier = pltpu.get_barrier_semaphore()

    def greet(device):
        pl.semaphore_signal(barrier, inc=1, device_id=device, device_id_type=MESH)

    @pl.loop(1, 64)
    def _(i):
        q = (me + i) % 64
        greet((q % 8, zh * 8 + q // 8))

    @pl.loop(0, 8)
    def _(k):
        greet((b, above + k))
        greet((b, below + k))

    greet((b, (zh + 2) % 4 * 8 + yc))
    for i in range(1, 4):
        greet((x * 2 + 1 - lower, (zh + i) % 4 * 8 + yc))

    r = lax.broadcasted_iota(jnp.int32, (128, 128), 0)
    c = lax.broadcasted_iota(jnp.int32, (128, 128), 1)
    apart = (r - c + 128) % 128
    near = jnp.where((apart == 1) | (apart == 127), 1.0, 0.0)
    far = jnp.where((apart == 2) | (apart == 126), SECOND, 0.0)
    for h in range(2):
        circulant[h * 128 : (h + 1) * 128] = (near + far).astype(bf16)

    loadp.wait()
    potb[...] = potv[...].astype(bf16)
    potp[yc] = potb[x]
    pl.semaphore_wait(barrier, 83)

    for i in range(1, 8):
        remote(potb.at[x], potp.at[yc], psem.at[0], psem.at[1], (b, zh * 8 + (yc + i) % 8)).start()

    @pl.when(yc < 3)
    def _():
        for k in range(8):
            remote(potb.at[x], poth.at[3 + yc], psem.at[2], psem.at[3], (b, below + k)).start()

    @pl.when(yc >= 5)
    def _():
        for k in range(8):
            remote(potb.at[x], poth.at[yc - 5], psem.at[2], psem.at[3], (b, above + k)).start()

    load.wait()

    def out_copy(k, o):
        return remote(send.at[o, k], rec.at[o, 3 + yc], ssem.at[o, k], rsem.at[o, 3 + yc], (b, zh * 8 + k))

    def in_copy(k, o):
        return remote(send.at[o, k], rec.at[o, 3 + k], ssem.at[o, 0], rsem.at[o, 3 + k], (b, zh * 8 + k))

    def down(k, o):
        return remote(rec.at[o, 3 + k], rec.at[o, 11 + k], fsem.at[o, k], rsem.at[o, 11 + k], (b, below + yc))

    def up(k, o):
        return remote(rec.at[o, 3 + k], rec.at[o, k - 5], fsem.at[o, k], rsem.at[o, k - 5], (b, above + yc))

    def along_x(i, src, dst, sem):
        return remote(src, dst, psem.at[sem], psem.at[sem + 1], ((x + i) % 4 * 2 + lower, d))

    for o in range(2):

        @pl.loop(1, 8)
        def _(i):
            k = (yc + i) % 8
            for j in range(4):
                send[o, k, j] = orb[2 * k + o, j].astype(bf16)
            out_copy(k, o).start()

        for j in range(4):
            rec[o, 3 + yc, j] = orb[2 * yc + o, j].astype(bf16)

        if o == 0:
            for i in range(1, 8):
                wait_bytes(send.at[0, 0], ssem.at[0, (yc + i) % 8])

    wait_bytes(potp.at[0:7], psem.at[1])
    for i in range(1, 4):
        along_x(i, potp, potg.at[x], 4).start()
    potg[x] = potp[...]
    wait_bytes(poth, psem.at[3])
    for i in range(1, 4):
        along_x(i, poth, poti.at[x], 6).start()
    poti[x] = poth[...]

    def receive(o):
        for k in (0, 7, 1, 6, 2, 5, 3, 4):

            @pl.when(yc != k)
            def _():
                in_copy(k, o).wait_recv()

            if k < 3:
                down(k, o).start()
            if k >= 5:
                up(k, o).start()
            unpack(3 + k, o, rec, levels[0])

    step = functools.partial(advance, levels=levels, pot=pot, circulant=circulant, sendf=sendf)
    receive(0)
    receive(1)
    wait_bytes(potg.at[0:3], psem.at[5])

    @pl.loop(0, 8)
    def _(s):
        for i in range(4):
            pot[12 + 4 * s + i] = scaled(potg[i, s])

    @pl.loop(0, 2)
    def _(o):
        for k in range(1, 7):
            step(k, o, [(12 + 2 * k, 32 - 4 * k)])

    own = pl.ds(b * 16 + yc * 2, 2)

    def deliver(to):
        @pl.loop(0, 8)
        def _(i):
            band = (b + i) % 8
            q = to * 8 + band

            @pl.when(q != me)
            def _():
                remote(sendf.at[q], gath.at[own], gsem.at[0], gsem.at[1], (band, zh * 8 + to)).start()

    deliver(3)
    deliver(4)

    wait_bytes(poti.at[0:3], psem.at[7])
    for s in range(3):
        for i in range(4):
            pot[4 * s + i] = scaled(poti[i, s])
            pot[44 + 4 * s + i] = scaled(poti[i, 3 + s])

    def halo(s, o):
        up(7 - s, o).wait_recv()
        down(s, o).wait_recv()
        unpack(2 - s, o, rec, levels[0])
        unpack(11 + s, o, rec, levels[0])

    for s in range(3):
        halo(s, 0)
    for k in range(1, 7):
        step(k, 0, [(2 * k, 12), (44 - 2 * k, 12)])

    @pl.loop(0, 3)
    def _(s):
        halo(s, 1)
        for k in range(1, 7):
            step(k, 1, [(8 - 4 * s + 2 * k, 4), (44 + 4 * s - 2 * k, 4)])
        deliver(2 - s)
        deliver(5 + s)

    gath[own] = sendf[me]

    wait_bytes(potp.at[0:7], psem.at[0])

    @pl.when((yc < 3) | (yc >= 5))
    def _():
        wait_bytes(potp, psem.at[2])

    wait_bytes(potg.at[0:3], psem.at[4])
    wait_bytes(poti.at[0:3], psem.at[6])
    for o in range(2):
        for i in range(1, 8):
            if o == 1:
                out_copy((yc + i) % 8, o).wait_send()
        for k in (0, 1, 2):
            down(k, o).wait_send()
        for k in (5, 6, 7):
            up(k, o).wait_send()
    wait_bytes(gath.at[0:126], gsem.at[1])

    t = jnp.swapaxes(gath[...].astype(f32), 0, 1).astype(bf16)
    t_ref[...] = t
    cells = jnp.concatenate([t[j] for j in range(16)], axis=1)
    gram = lax.dot_general(cells, cells, (((1,), (1,)), ((), ())), preferred_element_type=f32)
    part[...] = gram.reshape(32, 4, 128)
    mine, level = x * 8 + yc, zh * 2 + lower

    def among(i):
        j = (mine + i) % 32
        return j, (j // 8 * 2 + lower, zh * 8 + j % 8)

    @pl.loop(1, 32)
    def _(i):
        j, device = among(i)
        remote(part.at[j], r1.at[mine], asem.at[0], asem.at[1], device).start()

    r1[mine] = part[mine]
    wait_bytes(r1.at[0:31], asem.at[1])
    q1[...] = jnp.sum(r1[...], axis=0)
    for i in range(1, 8):
        j = (level + i) % 8
        remote(q1, r2.at[level], asem.at[2], asem.at[3], (x * 2 + j % 2, j // 2 * 8 + yc)).start()
    r2[level] = q1[...]
    wait_bytes(r2.at[0:7], asem.at[3])
    q2[...] = jnp.sum(r2[...], axis=0)

    @pl.loop(1, 32)
    def _(i):
        j, device = among(i)
        remote(q2, gram_ref.at[mine], asem.at[4], asem.at[5], device).start()

    gram_ref[mine] = q2[...]
    wait_bytes(gram_ref.at[0:31], asem.at[5])
    inverse = inverse_factor(gram_ref[...].reshape(128, 128) * (1.0 / 2.0**19))
    w = jnp.concatenate([block.astype(bf16) for block in inverse], axis=0)
    for j in range(16):
        rot[j] = jnp.dot(w, t_ref[j], preferred_element_type=f32)

    def turned(k):
        return jnp.swapaxes(rot[:, pl.ds(pl.multiple_of(16 * k, 16), 16), :], 0, 1).astype(bf16)

    def cells_of(band):
        return out_hbm.at[:, band // 2, pl.ds(pl.multiple_of(band % 2 * 16, 16), 16), :]

    def back_copy(i):
        k = (b + i) % 8
        return remote(sendr.at[k], cells_of(b), bsem.at[i], csem.at[b], (k, d))

    @pl.loop(1, 8)
    def _(i):
        k = (b + i) % 8
        sendr[k] = turned(k)
        back_copy(i).start()

    sendr[b] = turned(b)
    stay = pltpu.make_async_copy(sendr.at[b], cells_of(b), osem.at[0])
    stay.start()

    wait_bytes(gath.at[0:126], gsem.at[0])
    wait_bytes(r1.at[0:31], asem.at[0])
    wait_bytes(r2.at[0:7], asem.at[2])
    wait_bytes(r1.at[0:31], asem.at[4])
    for i in range(1, 8):
        back_copy(i).wait_send()
    for i in range(1, 8):
        k = (b + 8 - i) % 8
        remote(sendr.at[k], cells_of(k), bsem.at[0], csem.at[k], (k, d)).wait_recv()
    stay.wait()


def body(orbitals, potential):
    dma = pltpu.SemaphoreType.DMA
    rotated = pl.pallas_call(
        kernel,
        out_shape=jax.ShapeDtypeStruct((16, 4, 32, 128), bf16),
        in_specs=[ANY, ANY],
        out_specs=ANY,
        scratch_shapes=[
            pltpu.VMEM((16, 4, 32, 128), f32),
            pltpu.VMEM((4, 32, 128), f32),
            pltpu.VMEM((4, 32, 128), bf16),
            pltpu.VMEM((8, 32, 128), bf16),
            pltpu.VMEM((6, 32, 128), bf16),
            pltpu.VMEM((4, 8, 32, 128), bf16),
            pltpu.VMEM((4, 6, 32, 128), bf16),
            pltpu.VMEM((2, 8, 4, 32, 128), bf16),
            pltpu.VMEM((2, 14, 4, 32, 128), bf16),
            pltpu.VMEM((56, 32, 128), f32),
            pltpu.VMEM((256, 128), bf16),
            pltpu.VMEM((64, 2, 16, 128), bf16),
            pltpu.VMEM((128, 16, 128), bf16),
            pltpu.VMEM((32, 4, 128), f32),
            pltpu.VMEM((32, 4, 128), f32),
            pltpu.VMEM((4, 128), f32),
            pltpu.VMEM((8, 4, 128), f32),
            pltpu.VMEM((4, 128), f32),
            pltpu.VMEM((32, 4, 128), f32),
            pltpu.VMEM((16, 128, 128), bf16),
            pltpu.VMEM((16, 128, 128), f32),
            pltpu.VMEM((8, 16, 16, 128), bf16),
        ]
        + [pltpu.VMEM((56, 2, 48, 128), f32)] * 6
        + [dma((2,)), dma((8,)), dma((2, 8)), dma((2, 14)), dma((2, 8)), dma((2,)), dma((8,)), dma((8,)), dma((8,)), dma((8,))],
        compiler_params=pltpu.CompilerParams(collective_id=0, has_side_effects=True, vmem_limit_bytes=60 << 20),
    )(orbitals, potential)
    return rotated.astype(f32)


def solution(mesh):
    placed = (P("band", "dom", None, None), P("dom", None, None))
    return jax.shard_map(
        body, mesh=mesh, in_specs=placed, out_specs=P("band", "dom", None, None), check_vma=False
    )
```

```python
import functools

import jax
import jax.numpy as jnp
from jax import lax
from jax.experimental import pallas as pl
from jax.experimental.pallas import tpu as pltpu
from jax.sharding import PartitionSpec as P

MESH = pl.DeviceIdType.MESH
f32, bf16 = jnp.float32, jnp.bfloat16

centre = 5.5
half = 4.5
SCALE = 2.0 / half
DIAGONAL = 0.5 * 7.5 - centre
FIRST = -0.5 * (4.0 / 3.0) * SCALE
SECOND = -1.0 / 16.0

VMEM = pl.BlockSpec(memory_space=pltpu.VMEM)
ANY = pl.BlockSpec(memory_space=pl.ANY)


def remote(src, dst, send_sem, recv_sem, device):
    return pltpu.make_async_remote_copy(
        src_ref=src, dst_ref=dst, send_sem=send_sem, recv_sem=recv_sem, device_id=device, device_id_type=MESH
    )


def wait_bytes(ref, sem):
    pltpu.make_async_copy(ref, ref, sem).wait()


def put(dst, p, o, v):
    dst[p, o, 8:40] = v
    dst[p, o, 0:8] = v[24:32]
    dst[p, o, 40:48] = v[0:8]


def unpack(slot, o, rec, field):
    for i in range(4):
        put(field, 4 * slot + i, o, rec[o, slot, i].astype(f32))


def scaled(plane):
    return (plane.astype(f32) + DIAGONAL) * SCALE


def advance(k, o, segments, levels, pot, circulant, sendf):
    src, prev = levels[k - 1], levels[k - 2]
    for first, planes in segments:
        window = [src[first - 2 + j, o, 8:40] for j in range(planes + 4)]
        v = jnp.concatenate(window[2:-2], axis=0)
        high = v.astype(bf16)
        low = (v - high.astype(f32)).astype(bf16)
        z = jnp.dot(jnp.concatenate([high, low], axis=1), circulant[...], preferred_element_type=f32)
        for i in range(planes):
            p = first + i
            s1 = window[i + 1] + window[i + 3]
            s2 = window[i] + window[i + 4]
            s1 = s1 + (src[p, o, 7:39] + src[p, o, 9:41])
            s2 = s2 + (src[p, o, 6:38] + src[p, o, 10:42])
            w = pot[p] * window[i + 2] + (s1 + z[32 * i : 32 * i + 32] + s2 * SECOND) * FIRST
            w = w * 0.5 if k == 1 else w - prev[p, o, 8:40]
            if k < 6:
                put(levels[k], p, o, w)
            else:
                w = w.astype(bf16)
                sendf[2 * (p - 12), o] = w[0:16]
                sendf[2 * (p - 12) + 1, o] = w[16:32]


def inverse_factor(m):
    n, nb = 128, 16
    row = lax.broadcasted_iota(jnp.int32, (nb, n), 0)
    lane = lax.broadcasted_iota(jnp.int32, (nb, n), 1)
    out = []
    for k in range(n // nb):
        at, lo = k * nb, (k + 1) * nb
        x = m[at:lo]
        cols = [jnp.broadcast_to(x[:, at + t : at + t + 1], (nb, n)) for t in range(nb)]
        own = (lane >= at) & (lane < lo)
        x = jnp.where(own, jnp.where(lane - at == row, 1.0, 0.0), x)
        w = jnp.zeros_like(x)
        for t in range(nb):
            here = row == t
            pivot = jnp.broadcast_to(cols[t][t : t + 1], (nb, n))
            inv = 1.0 / pivot
            r = jnp.broadcast_to(x[t : t + 1], (nb, n))
            w = jnp.where(here, r * lax.rsqrt(pivot), w)
            mult = jnp.where(here, 1.0 - inv, cols[t] * inv)
            x = x - mult * r
            for u in range(t + 1, nb):
                cols[u] = cols[u] - mult * jnp.broadcast_to(cols[u][t : t + 1], (nb, n))
        out.append(jnp.where(lane < lo, w, 0.0))
        if lo < n:
            below = m[lo:]
            lane_b = lax.broadcasted_iota(jnp.int32, below.shape, 1)
            padded = [jnp.zeros((at, n), f32)] * (at > 0) + [x, jnp.zeros((n - lo, n), f32)]
            change = jnp.dot(
                below, jnp.concatenate(padded, 0), precision=lax.Precision.HIGHEST, preferred_element_type=f32
            )
            kept = jnp.where((lane_b >= at) & (lane_b < lo), 0.0, below)
            m = jnp.concatenate([m[:lo], kept - change], axis=0)
    return out


def kernel(
    orb_hbm, pot_hbm, out_hbm,
    orb, potv, potb, potp, poth, potg, poti, send, rec, pot, circulant, sendf, gath,
    part, r1, q1, r2, q2, gram_ref, t_ref, rot, sendr, *rest
):
    levels, (lsem, psem, ssem, rsem, fsem, dsem, gsem, asem, bsem, csem, osem) = rest[:6], rest[6:]
    b, d = lax.axis_index("band"), lax.axis_index("dom")
    yc, zh = d % 8, d // 8
    x, lower = b // 2, b % 2
    me = yc * 8 + b
    above, below = (zh + 1) % 4 * 8, (zh + 3) % 4 * 8

    loadp = pltpu.make_async_copy(pot_hbm, potv, lsem.at[1])
    loadp.start()
    load = pltpu.make_async_copy(orb_hbm, orb, lsem.at[0])
    load.start()

    barrier = pltpu.get_barrier_semaphore()

    def greet(device):
        pl.semaphore_signal(barrier, inc=1, device_id=device, device_id_type=MESH)

    for i in range(1, 8):
        greet((b, zh * 8 + (yc + i) % 8))

    @pl.loop(0, 8)
    def _(k):
        greet((b, above + k))
        greet((b, below + k))

    @pl.loop(8, 64)
    def _(i):
        greet(((b + i // 8) % 8, zh * 8 + i % 8))

    greet((b, (zh + 2) % 4 * 8 + yc))
    for i in range(1, 4):
        greet((x * 2 + 1 - lower, (zh + i) % 4 * 8 + yc))

    r = lax.broadcasted_iota(jnp.int32, (128, 128), 0)
    c = lax.broadcasted_iota(jnp.int32, (128, 128), 1)
    apart = (r - c + 128) % 128
    near = jnp.where((apart == 1) | (apart == 127), 1.0, 0.0)
    far = jnp.where((apart == 2) | (apart == 126), SECOND, 0.0)
    for h in range(2):
        circulant[h * 128 : (h + 1) * 128] = (near + far).astype(bf16)

    loadp.wait()
    potb[...] = potv[...].astype(bf16)
    potp[yc] = potb[x]
    pl.semaphore_wait(barrier, 83)

    for i in range(1, 8):
        remote(potb.at[x], potp.at[yc], psem.at[0], psem.at[1], (b, zh * 8 + (yc + i) % 8)).start()

    @pl.when(yc < 3)
    def _():
        for k in range(8):
            remote(potb.at[x], poth.at[3 + yc], psem.at[2], psem.at[3], (b, below + k)).start()

    @pl.when(yc >= 5)
    def _():
        for k in range(8):
            remote(potb.at[x], poth.at[yc - 5], psem.at[2], psem.at[3], (b, above + k)).start()

    load.wait()

    def out_copy(k, o):
        return remote(send.at[o, k], rec.at[o, 3 + yc], ssem.at[o, k], rsem.at[o, 3 + yc], (b, zh * 8 + k))

    def in_copy(k, o):
        return remote(send.at[o, k], rec.at[o, 3 + k], ssem.at[o, 0], rsem.at[o, 3 + k], (b, zh * 8 + k))

    def down(k, o):
        return remote(rec.at[o, 3 + k], rec.at[o, 11 + k], fsem.at[o, k], rsem.at[o, 11 + k], (b, below + yc))

    def up(k, o):
        return remote(rec.at[o, 3 + k], rec.at[o, k - 5], fsem.at[o, k], rsem.at[o, k - 5], (b, above + yc))

    sibling = yc + 1 - 2 * (yc % 2)

    def straight_down(k, o, i):
        return remote(send.at[o, k], rec.at[o, 11 + yc], dsem.at[o, i], rsem.at[o, 11 + yc], (b, below + k))

    def straight_up(k, o, i):
        return remote(send.at[o, k], rec.at[o, yc - 5], dsem.at[o, i], rsem.at[o, yc - 5], (b, above + k))

    def along_x(i, src, dst, sem):
        return remote(src, dst, psem.at[sem], psem.at[sem + 1], ((x + i) % 4 * 2 + lower, d))

    for o in range(2):

        for k in (yc, sibling):
            for j in range(4):
                send[o, k, j] = orb[2 * k + o, j].astype(bf16)

        @pl.when(yc < 3)
        def _():
            straight_down(yc, o, 0).start()
            straight_down(sibling, o, 1).start()

        @pl.when(yc >= 5)
        def _():
            straight_up(yc, o, 0).start()
            straight_up(sibling, o, 1).start()

        @pl.loop(1, 8)
        def _(i):
            k = (yc + i) % 8

            @pl.when(k != sibling)
            def _():
                for j in range(4):
                    send[o, k, j] = orb[2 * k + o, j].astype(bf16)

            out_copy(k, o).start()

        rec[o, 3 + yc] = send[o, yc]

        if o == 0:
            for i in range(1, 8):
                wait_bytes(send.at[0, 0], ssem.at[0, (yc + i) % 8])

    wait_bytes(potp.at[0:7], psem.at[1])
    for i in range(1, 4):
        along_x(i, potp, potg.at[x], 4).start()
    potg[x] = potp[...]
    wait_bytes(poth, psem.at[3])
    for i in range(1, 4):
        along_x(i, poth, poti.at[x], 6).start()
    poti[x] = poth[...]

    def forward(k, o):
        @pl.when(yc // 2 != k // 2)
        def _():
            (down if k < 3 else up)(k, o).start()

    def receive(o, to_forward):
        for k in (0, 7, 1, 6, 2, 5, 3, 4):

            @pl.when(yc != k)
            def _():
                in_copy(k, o).wait_recv()

            if k in to_forward:
                forward(k, o)
            unpack(3 + k, o, rec, levels[0])

    step = functools.partial(advance, levels=levels, pot=pot, circulant=circulant, sendf=sendf)

    def inner(o):
        for k in range(1, 7):
            step(k, o, [(12 + 2 * k, 32 - 4 * k)])

    own = b * 16 + yc * 2

    def deliver(to, orbitals=(0, 1)):
        @pl.loop(0, 8)
        def _(i):
            band = (b + 4 + i) % 8
            q = to * 8 + band
            part_of = pl.ds(orbitals[0], len(orbitals))

            @pl.when(q != me)
            def _():
                remote(
                    sendf.at[q, part_of],
                    gath.at[pl.ds(own + orbitals[0], len(orbitals))],
                    gsem.at[0],
                    gsem.at[1],
                    (band, zh * 8 + to),
                ).start()

    def halo(s, o):
        up(7 - s, o).wait_recv()
        down(s, o).wait_recv()
        unpack(2 - s, o, rec, levels[0])
        unpack(11 + s, o, rec, levels[0])

    def piece(s):
        for k in range(1, 7):
            step(k, 1, [(8 - 4 * s + 2 * k, 4), (44 + 4 * s - 2 * k, 4)])

    receive(0, (0, 7, 1, 6, 2, 5))
    receive(1, (0, 7, 1, 6))
    wait_bytes(potg.at[0:3], psem.at[5])

    @pl.loop(0, 8)
    def _(s):
        for i in range(4):
            pot[12 + 4 * s + i] = scaled(potg[i, s])

    inner(0)
    forward(2, 1)
    forward(5, 1)
    inner(1)
    deliver(3)
    deliver(4)

    wait_bytes(poti.at[0:3], psem.at[7])
    for s in range(3):
        for i in range(4):
            pot[4 * s + i] = scaled(poti[i, s])
            pot[44 + 4 * s + i] = scaled(poti[i, 3 + s])

    for s in range(3):
        halo(s, 0)
    for k in range(1, 7):
        step(k, 0, [(2 * k, 12), (44 - 2 * k, 12)])
    deliver(0, (0,))
    deliver(7, (0,))

    @pl.loop(0, 2)
    def _(s):
        halo(s, 1)
        piece(s)
        deliver(2 - s)
        deliver(5 + s)

    halo(2, 1)
    piece(2)
    deliver(0, (1,))
    deliver(7, (1,))

    gath[pl.ds(own, 2)] = sendf[me]

    wait_bytes(potp.at[0:7], psem.at[0])

    @pl.when((yc < 3) | (yc >= 5))
    def _():
        wait_bytes(potp, psem.at[2])

    wait_bytes(potg.at[0:3], psem.at[4])
    wait_bytes(poti.at[0:3], psem.at[6])
    for o in range(2):
        for i in range(1, 8):
            if o == 1:
                out_copy((yc + i) % 8, o).wait_send()
        for k in (0, 1, 2, 5, 6, 7):

            @pl.when(yc // 2 != k // 2)
            def _():
                wait_bytes(send.at[0, 0], fsem.at[o, k])

        @pl.when((yc < 3) | (yc >= 5))
        def _():
            for i in range(2):
                wait_bytes(send.at[0, 0], dsem.at[o, i])

    wait_bytes(gath.at[0:126], gsem.at[1])

    t = jnp.swapaxes(gath[...].astype(f32), 0, 1).astype(bf16)
    t_ref[...] = t
    cells = jnp.concatenate([t[j] for j in range(16)], axis=1)
    gram = lax.dot_general(cells, cells, (((1,), (1,)), ((), ())), preferred_element_type=f32)
    part[...] = gram.reshape(32, 4, 128)
    mine, level = x * 8 + yc, zh * 2 + lower

    def others(send_to):
        @pl.loop(0, 32)
        def _(i):
            col, row = (x + i // 8 + 2) % 4, (yc + i + 4) % 8

            @pl.when(i != 20)
            def _():
                send_to(col * 8 + row, (col * 2 + lower, zh * 8 + row))

    @others
    def _(j, device):
        remote(part.at[j], r1.at[mine], asem.at[0], asem.at[1], device).start()

    r1[mine] = part[mine]
    wait_bytes(r1.at[0:31], asem.at[1])
    q1[...] = jnp.sum(r1[...], axis=0)
    for i in (4, 3, 5, 2, 6, 1, 7):
        j = (level + i) % 8
        remote(q1, r2.at[level], asem.at[2], asem.at[3], (x * 2 + j % 2, j // 2 * 8 + yc)).start()
    r2[level] = q1[...]
    wait_bytes(r2.at[0:7], asem.at[3])
    q2[...] = jnp.sum(r2[...], axis=0)

    @others
    def _(j, device):
        remote(q2, gram_ref.at[mine], asem.at[4], asem.at[5], device).start()

    gram_ref[mine] = q2[...]
    wait_bytes(gram_ref.at[0:31], asem.at[5])
    inverse = inverse_factor(gram_ref[...].reshape(128, 128) * (1.0 / 2.0**19))
    w = jnp.concatenate([block.astype(bf16) for block in inverse], axis=0)
    for j in range(16):
        rot[j] = jnp.dot(w, t_ref[j], preferred_element_type=f32)

    def turned(k):
        return jnp.swapaxes(rot[:, pl.ds(pl.multiple_of(16 * k, 16), 16), :], 0, 1).astype(bf16)

    def cells_of(band):
        return out_hbm.at[:, band // 2, pl.ds(pl.multiple_of(band % 2 * 16, 16), 16), :]

    def back_copy(i):
        k = (b + i) % 8
        return remote(sendr.at[k], cells_of(b), bsem.at[i], csem.at[b], (k, d))

    @pl.loop(1, 8)
    def _(i):
        k = (b + i) % 8
        sendr[k] = turned(k)
        back_copy(i).start()

    sendr[b] = turned(b)
    stay = pltpu.make_async_copy(sendr.at[b], cells_of(b), osem.at[0])
    stay.start()

    wait_bytes(gath.at[0:126], gsem.at[0])
    wait_bytes(r1.at[0:31], asem.at[0])
    wait_bytes(r2.at[0:7], asem.at[2])
    wait_bytes(r1.at[0:31], asem.at[4])
    for i in range(1, 8):
        back_copy(i).wait_send()
    for i in range(1, 8):
        k = (b + 8 - i) % 8
        remote(sendr.at[k], cells_of(k), bsem.at[0], csem.at[k], (k, d)).wait_recv()
    stay.wait()


def body(orbitals, potential):
    dma = pltpu.SemaphoreType.DMA
    rotated = pl.pallas_call(
        kernel,
        out_shape=jax.ShapeDtypeStruct((16, 4, 32, 128), bf16),
        in_specs=[ANY, ANY],
        out_specs=ANY,
        scratch_shapes=[
            pltpu.VMEM((16, 4, 32, 128), f32),
            pltpu.VMEM((4, 32, 128), f32),
            pltpu.VMEM((4, 32, 128), bf16),
            pltpu.VMEM((8, 32, 128), bf16),
            pltpu.VMEM((6, 32, 128), bf16),
            pltpu.VMEM((4, 8, 32, 128), bf16),
            pltpu.VMEM((4, 6, 32, 128), bf16),
            pltpu.VMEM((2, 8, 4, 32, 128), bf16),
            pltpu.VMEM((2, 14, 4, 32, 128), bf16),
            pltpu.VMEM((56, 32, 128), f32),
            pltpu.VMEM((256, 128), bf16),
            pltpu.VMEM((64, 2, 16, 128), bf16),
            pltpu.VMEM((128, 16, 128), bf16),
            pltpu.VMEM((32, 4, 128), f32),
            pltpu.VMEM((32, 4, 128), f32),
            pltpu.VMEM((4, 128), f32),
            pltpu.VMEM((8, 4, 128), f32),
            pltpu.VMEM((4, 128), f32),
            pltpu.VMEM((32, 4, 128), f32),
            pltpu.VMEM((16, 128, 128), bf16),
            pltpu.VMEM((16, 128, 128), f32),
            pltpu.VMEM((8, 16, 16, 128), bf16),
        ]
        + [pltpu.VMEM((56, 2, 48, 128), f32)] * 6
        + [dma((2,)), dma((8,)), dma((2, 8)), dma((2, 14)), dma((2, 8)), dma((2, 2)), dma((2,)), dma((8,)), dma((8,)), dma((8,)), dma((8,))],
        compiler_params=pltpu.CompilerParams(collective_id=0, has_side_effects=True, vmem_limit_bytes=60 << 20),
    )(orbitals, potential)
    return rotated.astype(f32)


def solution(mesh):
    placed = (P("band", "dom", None, None), P("dom", None, None))
    return jax.shard_map(
        body, mesh=mesh, in_specs=placed, out_specs=P("band", "dom", None, None), check_vma=False
    )
```

```python
import functools

import jax
import jax.numpy as jnp
from jax import lax
from jax.experimental import pallas as pl
from jax.experimental.pallas import tpu as pltpu
from jax.sharding import PartitionSpec as P

MESH = pl.DeviceIdType.MESH
f32, bf16 = jnp.float32, jnp.bfloat16

centre = 5.5
half = 4.5
SCALE = 2.0 / half
DIAGONAL = 0.5 * 7.5 - centre
FIRST = -0.5 * (4.0 / 3.0) * SCALE
SECOND = -1.0 / 16.0

VMEM = pl.BlockSpec(memory_space=pltpu.VMEM)
ANY = pl.BlockSpec(memory_space=pl.ANY)


def remote(src, dst, send_sem, recv_sem, device):
    return pltpu.make_async_remote_copy(
        src_ref=src, dst_ref=dst, send_sem=send_sem, recv_sem=recv_sem, device_id=device, device_id_type=MESH
    )


def wait_bytes(ref, sem):
    pltpu.make_async_copy(ref, ref, sem).wait()


def put(dst, p, o, v):
    dst[p, o, 8:40] = v
    dst[p, o, 0:8] = v[24:32]
    dst[p, o, 40:48] = v[0:8]


def unpack(slot, o, rec, field):
    for i in range(4):
        put(field, 4 * slot + i, o, rec[o, slot, i].astype(f32))


def scaled(plane):
    return (plane.astype(f32) + DIAGONAL) * SCALE


def advance(k, o, segments, levels, pot, circulant, sendf):
    src, prev = levels[k - 1], levels[k - 2]
    for first, planes in segments:
        window = [src[first - 2 + j, o, 8:40] for j in range(planes + 4)]
        v = jnp.concatenate(window[2:-2], axis=0)
        high = v.astype(bf16)
        low = (v - high.astype(f32)).astype(bf16)
        z = jnp.dot(jnp.concatenate([high, low], axis=1), circulant[...], preferred_element_type=f32)
        for i in range(planes):
            p = first + i
            s1 = window[i + 1] + window[i + 3]
            s2 = window[i] + window[i + 4]
            s1 = s1 + (src[p, o, 7:39] + src[p, o, 9:41])
            s2 = s2 + (src[p, o, 6:38] + src[p, o, 10:42])
            w = pot[p] * window[i + 2] + (s1 + z[32 * i : 32 * i + 32] + s2 * SECOND) * FIRST
            w = w * 0.5 if k == 1 else w - prev[p, o, 8:40]
            if k < 6:
                put(levels[k], p, o, w)
            else:
                w = w.astype(bf16)
                sendf[2 * (p - 12), o] = w[0:16]
                sendf[2 * (p - 12) + 1, o] = w[16:32]


def inverse_factor(m):
    n, nb = 128, 16
    row = lax.broadcasted_iota(jnp.int32, (nb, n), 0)
    lane = lax.broadcasted_iota(jnp.int32, (nb, n), 1)
    out = []
    for k in range(n // nb):
        at, lo = k * nb, (k + 1) * nb
        x = m[at:lo]
        cols = [jnp.broadcast_to(x[:, at + t : at + t + 1], (nb, n)) for t in range(nb)]
        own = (lane >= at) & (lane < lo)
        x = jnp.where(own, jnp.where(lane - at == row, 1.0, 0.0), x)
        w = jnp.zeros_like(x)
        for t in range(nb):
            here = row == t
            pivot = jnp.broadcast_to(cols[t][t : t + 1], (nb, n))
            inv = 1.0 / pivot
            r = jnp.broadcast_to(x[t : t + 1], (nb, n))
            w = jnp.where(here, r * lax.rsqrt(pivot), w)
            mult = jnp.where(here, 1.0 - inv, cols[t] * inv)
            x = x - mult * r
            for u in range(t + 1, nb):
                cols[u] = cols[u] - mult * jnp.broadcast_to(cols[u][t : t + 1], (nb, n))
        out.append(jnp.where(lane < lo, w, 0.0))
        if lo < n:
            below = m[lo:]
            lane_b = lax.broadcasted_iota(jnp.int32, below.shape, 1)
            padded = [jnp.zeros((at, n), f32)] * (at > 0) + [x, jnp.zeros((n - lo, n), f32)]
            change = jnp.dot(
                below, jnp.concatenate(padded, 0), precision=lax.Precision.HIGHEST, preferred_element_type=f32
            )
            kept = jnp.where((lane_b >= at) & (lane_b < lo), 0.0, below)
            m = jnp.concatenate([m[:lo], kept - change], axis=0)
    return out


def kernel(
    orb_hbm, pot_hbm, out_hbm,
    orb, potv, potb, potp, poth, potg, poti, send, rec, pot, circulant, sendf, gath,
    part, r1, q1, r2, q2, gram_ref, t_ref, rot, sendr, *rest
):
    levels, (lsem, psem, ssem, rsem, fsem, dsem, gsem, asem, bsem, csem, osem, ready) = rest[:6], rest[6:]
    b, d = lax.axis_index("band"), lax.axis_index("dom")
    yc, zh = d % 8, d // 8
    x, lower = b // 2, b % 2
    me = yc * 8 + b
    above, below = (zh + 1) % 4 * 8, (zh + 3) % 4 * 8

    loadp = pltpu.make_async_copy(pot_hbm, potv, lsem.at[1])
    loadp.start()
    load = pltpu.make_async_copy(orb_hbm, orb, lsem.at[0])
    load.start()

    barrier = pltpu.get_barrier_semaphore()

    def greet(device):
        pl.semaphore_signal(barrier, inc=1, device_id=device, device_id_type=MESH)

    for i in range(1, 8):
        greet((b, zh * 8 + (yc + i) % 8))

    @pl.loop(0, 8)
    def _(k):
        greet((b, above + k))
        greet((b, below + k))

    for i in range(1, 8):
        greet(((b + i) % 8, d))
    greet((b, (zh + 2) % 4 * 8 + yc))
    for i in range(1, 4):
        greet((x * 2 + 1 - lower, (zh + i) % 4 * 8 + yc))

    r = lax.broadcasted_iota(jnp.int32, (128, 128), 0)
    c = lax.broadcasted_iota(jnp.int32, (128, 128), 1)
    apart = (r - c + 128) % 128
    near = jnp.where((apart == 1) | (apart == 127), 1.0, 0.0)
    far = jnp.where((apart == 2) | (apart == 126), SECOND, 0.0)
    for h in range(2):
        circulant[h * 128 : (h + 1) * 128] = (near + far).astype(bf16)

    loadp.wait()
    potb[...] = potv[...].astype(bf16)
    potp[yc] = potb[x]
    load.wait()

    @pl.loop(0, 8)
    def _(k):
        for o in range(2):
            for j in range(4):
                send[o, k, j] = orb[2 * k + o, j].astype(bf16)

    pl.semaphore_wait(barrier, 34)

    for i in range(1, 8):
        remote(potb.at[x], potp.at[yc], psem.at[0], psem.at[1], (b, zh * 8 + (yc + i) % 8)).start()

    def halo_planes():
        @pl.when(yc < 3)
        def _():
            for k in range(8):
                remote(potb.at[x], poth.at[3 + yc], psem.at[2], psem.at[3], (b, below + k)).start()

        @pl.when(yc >= 5)
        def _():
            for k in range(8):
                remote(potb.at[x], poth.at[yc - 5], psem.at[2], psem.at[3], (b, above + k)).start()

    def out_copy(k, o):
        return remote(send.at[o, k], rec.at[o, 3 + yc], ssem.at[o, k], rsem.at[o, 3 + yc], (b, zh * 8 + k))

    def in_copy(k, o):
        return remote(send.at[o, k], rec.at[o, 3 + k], ssem.at[o, 0], rsem.at[o, 3 + k], (b, zh * 8 + k))

    def down(k, o):
        return remote(rec.at[o, 3 + k], rec.at[o, 11 + k], fsem.at[o, k], rsem.at[o, 11 + k], (b, below + yc))

    def up(k, o):
        return remote(rec.at[o, 3 + k], rec.at[o, k - 5], fsem.at[o, k], rsem.at[o, k - 5], (b, above + yc))

    sibling = yc + 1 - 2 * (yc % 2)

    def straight_down(k, o, i):
        return remote(send.at[o, k], rec.at[o, 11 + yc], dsem.at[o, i], rsem.at[o, 11 + yc], (b, below + k))

    def straight_up(k, o, i):
        return remote(send.at[o, k], rec.at[o, yc - 5], dsem.at[o, i], rsem.at[o, yc - 5], (b, above + k))

    def along_x(i, src, dst, sem):
        return remote(src, dst, psem.at[sem], psem.at[sem + 1], ((x + i) % 4 * 2 + lower, d))

    for o in range(2):

        @pl.when(yc < 3)
        def _():
            straight_down(yc, o, 0).start()
            straight_down(sibling, o, 1).start()

        @pl.when(yc >= 5)
        def _():
            straight_up(yc, o, 0).start()
            straight_up(sibling, o, 1).start()

        for i in (4, 3, 5, 2, 6, 1, 7):
            out_copy((yc + i) % 8, o).start()
        rec[o, 3 + yc] = send[o, yc]

        if o == 0:
            halo_planes()

            for i in range(1, 8):
                pl.semaphore_signal(ready, inc=1, device_id=((b + i) % 8, d), device_id_type=MESH)
            for i in range(1, 8):
                wait_bytes(send.at[0, 0], ssem.at[0, (yc + i) % 8])

    wait_bytes(potp.at[0:7], psem.at[1])
    for i in range(1, 4):
        along_x(i, potp, potg.at[x], 4).start()
    potg[x] = potp[...]
    wait_bytes(poth, psem.at[3])
    for i in range(1, 4):
        along_x(i, poth, poti.at[x], 6).start()
    poti[x] = poth[...]

    def forward(k, o):
        @pl.when(yc // 2 != k // 2)
        def _():
            (down if k < 3 else up)(k, o).start()

    def receive(o, to_forward):
        for k in (0, 7, 1, 6, 2, 5, 3, 4):

            @pl.when(yc != k)
            def _():
                in_copy(k, o).wait_recv()

            if k in to_forward:
                forward(k, o)
            unpack(3 + k, o, rec, levels[0])

    step = functools.partial(advance, levels=levels, pot=pot, circulant=circulant, sendf=sendf)

    def inner(o):
        for k in range(1, 7):
            step(k, o, [(12 + 2 * k, 32 - 4 * k)])

    own = b * 16 + yc * 2

    def deliver(to, orbitals=(0, 1)):
        @pl.loop(0, 8)
        def _(i):
            band = (b + 4 + i) % 8
            q = to * 8 + band
            part_of = pl.ds(orbitals[0], len(orbitals))

            @pl.when(q != me)
            def _():
                remote(
                    sendf.at[q, part_of],
                    gath.at[pl.ds(own + orbitals[0], len(orbitals))],
                    gsem.at[0],
                    gsem.at[1],
                    (band, zh * 8 + to),
                ).start()

    def halo(s, o):
        up(7 - s, o).wait_recv()
        down(s, o).wait_recv()
        unpack(2 - s, o, rec, levels[0])
        unpack(11 + s, o, rec, levels[0])

    def piece(s):
        for k in range(1, 7):
            step(k, 1, [(8 - 4 * s + 2 * k, 4), (44 + 4 * s - 2 * k, 4)])

    receive(0, (0, 7, 1, 6, 2, 5))
    receive(1, (0, 7, 1, 6))
    wait_bytes(potg.at[0:3], psem.at[5])

    @pl.loop(0, 8)
    def _(s):
        for i in range(4):
            pot[12 + 4 * s + i] = scaled(potg[i, s])

    inner(0)
    forward(2, 1)
    forward(5, 1)
    inner(1)
    pl.semaphore_wait(ready, 7)
    deliver(3)
    deliver(4)

    wait_bytes(poti.at[0:3], psem.at[7])
    for s in range(3):
        for i in range(4):
            pot[4 * s + i] = scaled(poti[i, s])
            pot[44 + 4 * s + i] = scaled(poti[i, 3 + s])

    for s in range(3):
        halo(s, 0)
    for k in range(1, 7):
        step(k, 0, [(2 * k, 12), (44 - 2 * k, 12)])
    deliver(0, (0,))
    deliver(7, (0,))

    @pl.loop(0, 2)
    def _(s):
        halo(s, 1)
        piece(s)
        deliver(2 - s)
        deliver(5 + s)

    halo(2, 1)
    piece(2)
    deliver(0, (1,))
    deliver(7, (1,))

    gath[pl.ds(own, 2)] = sendf[me]

    wait_bytes(potp.at[0:7], psem.at[0])

    @pl.when((yc < 3) | (yc >= 5))
    def _():
        wait_bytes(potp, psem.at[2])

    wait_bytes(potg.at[0:3], psem.at[4])
    wait_bytes(poti.at[0:3], psem.at[6])
    for o in range(2):
        for i in range(1, 8):
            if o == 1:
                out_copy((yc + i) % 8, o).wait_send()
        for k in (0, 1, 2, 5, 6, 7):

            @pl.when(yc // 2 != k // 2)
            def _():
                wait_bytes(send.at[0, 0], fsem.at[o, k])

        @pl.when((yc < 3) | (yc >= 5))
        def _():
            for i in range(2):
                wait_bytes(send.at[0, 0], dsem.at[o, i])

    wait_bytes(gath.at[0:126], gsem.at[1])

    t = jnp.swapaxes(gath[...].astype(f32), 0, 1).astype(bf16)
    t_ref[...] = t
    cells = jnp.concatenate([t[j] for j in range(16)], axis=1)
    gram = lax.dot_general(cells, cells, (((1,), (1,)), ((), ())), preferred_element_type=f32)
    part[...] = gram.reshape(32, 4, 128)
    mine, level = x * 8 + yc, zh * 2 + lower

    def others(send_to):
        @pl.loop(0, 32)
        def _(i):
            col, row = (x + i // 8 + 2) % 4, (yc + i + 4) % 8

            @pl.when(i != 20)
            def _():
                send_to(col * 8 + row, (col * 2 + lower, zh * 8 + row))

    @others
    def _(j, device):
        remote(part.at[j], r1.at[mine], asem.at[0], asem.at[1], device).start()

    r1[mine] = part[mine]
    wait_bytes(r1.at[0:31], asem.at[1])
    q1[...] = jnp.sum(r1[...], axis=0)
    for i in (4, 3, 5, 2, 6, 1, 7):
        j = (level + i) % 8
        remote(q1, r2.at[level], asem.at[2], asem.at[3], (x * 2 + j % 2, j // 2 * 8 + yc)).start()
    r2[level] = q1[...]
    wait_bytes(r2.at[0:7], asem.at[3])
    q2[...] = jnp.sum(r2[...], axis=0)

    @others
    def _(j, device):
        remote(q2, gram_ref.at[mine], asem.at[4], asem.at[5], device).start()

    gram_ref[mine] = q2[...]
    wait_bytes(gram_ref.at[0:31], asem.at[5])
    inverse = inverse_factor(gram_ref[...].reshape(128, 128) * (1.0 / 2.0**19))
    w = jnp.concatenate([block.astype(bf16) for block in inverse], axis=0)
    for j in range(16):
        rot[j] = jnp.dot(w, t_ref[j], preferred_element_type=f32)

    def turned(k):
        return jnp.swapaxes(rot[:, pl.ds(pl.multiple_of(16 * k, 16), 16), :], 0, 1).astype(bf16)

    def cells_of(band):
        return out_hbm.at[:, band // 2, pl.ds(pl.multiple_of(band % 2 * 16, 16), 16), :]

    def back_copy(i):
        k = (b + i) % 8
        return remote(sendr.at[k], cells_of(b), bsem.at[i], csem.at[b], (k, d))

    @pl.loop(1, 8)
    def _(i):
        k = (b + i) % 8
        sendr[k] = turned(k)
        back_copy(i).start()

    sendr[b] = turned(b)
    stay = pltpu.make_async_copy(sendr.at[b], cells_of(b), osem.at[0])
    stay.start()

    wait_bytes(gath.at[0:126], gsem.at[0])
    wait_bytes(r1.at[0:31], asem.at[0])
    wait_bytes(r2.at[0:7], asem.at[2])
    wait_bytes(r1.at[0:31], asem.at[4])
    for i in range(1, 8):
        back_copy(i).wait_send()
    for i in range(1, 8):
        k = (b + 8 - i) % 8
        remote(sendr.at[k], cells_of(k), bsem.at[0], csem.at[k], (k, d)).wait_recv()
    stay.wait()


def body(orbitals, potential):
    dma = pltpu.SemaphoreType.DMA
    rotated = pl.pallas_call(
        kernel,
        out_shape=jax.ShapeDtypeStruct((16, 4, 32, 128), bf16),
        in_specs=[ANY, ANY],
        out_specs=ANY,
        scratch_shapes=[
            pltpu.VMEM((16, 4, 32, 128), f32),
            pltpu.VMEM((4, 32, 128), f32),
            pltpu.VMEM((4, 32, 128), bf16),
            pltpu.VMEM((8, 32, 128), bf16),
            pltpu.VMEM((6, 32, 128), bf16),
            pltpu.VMEM((4, 8, 32, 128), bf16),
            pltpu.VMEM((4, 6, 32, 128), bf16),
            pltpu.VMEM((2, 8, 4, 32, 128), bf16),
            pltpu.VMEM((2, 14, 4, 32, 128), bf16),
            pltpu.VMEM((56, 32, 128), f32),
            pltpu.VMEM((256, 128), bf16),
            pltpu.VMEM((64, 2, 16, 128), bf16),
            pltpu.VMEM((128, 16, 128), bf16),
            pltpu.VMEM((32, 4, 128), f32),
            pltpu.VMEM((32, 4, 128), f32),
            pltpu.VMEM((4, 128), f32),
            pltpu.VMEM((8, 4, 128), f32),
            pltpu.VMEM((4, 128), f32),
            pltpu.VMEM((32, 4, 128), f32),
            pltpu.VMEM((16, 128, 128), bf16),
            pltpu.VMEM((16, 128, 128), f32),
            pltpu.VMEM((8, 16, 16, 128), bf16),
        ]
        + [pltpu.VMEM((56, 2, 48, 128), f32)] * 6
        + [dma((2,)), dma((8,)), dma((2, 8)), dma((2, 14)), dma((2, 8)), dma((2, 2)), dma((2,)), dma((8,)), dma((8,)), dma((8,)), dma((8,)), pltpu.SemaphoreType.REGULAR],
        compiler_params=pltpu.CompilerParams(collective_id=0, has_side_effects=True, vmem_limit_bytes=60 << 20),
    )(orbitals, potential)
    return rotated.astype(f32)


def solution(mesh):
    placed = (P("band", "dom", None, None), P("dom", None, None))
    return jax.shard_map(
        body, mesh=mesh, in_specs=placed, out_specs=P("band", "dom", None, None), check_vma=False
    )
```

```python
import functools

import jax
import jax.numpy as jnp
from jax import lax
from jax.experimental import pallas as pl
from jax.experimental.pallas import tpu as pltpu
from jax.sharding import PartitionSpec as P

MESH = pl.DeviceIdType.MESH
f32, bf16 = jnp.float32, jnp.bfloat16

centre = 5.5
half = 4.5
SCALE = 2.0 / half
DIAGONAL = 0.5 * 7.5 - centre
FIRST = -0.5 * (4.0 / 3.0) * SCALE
SECOND = -1.0 / 16.0

VMEM = pl.BlockSpec(memory_space=pltpu.VMEM)
ANY = pl.BlockSpec(memory_space=pl.ANY)


def remote(src, dst, send_sem, recv_sem, device):
    return pltpu.make_async_remote_copy(
        src_ref=src, dst_ref=dst, send_sem=send_sem, recv_sem=recv_sem, device_id=device, device_id_type=MESH
    )


def wait_bytes(ref, sem):
    pltpu.make_async_copy(ref, ref, sem).wait()


def put(dst, p, o, v):
    dst[p, o, 8:40] = v
    dst[p, o, 0:8] = v[24:32]
    dst[p, o, 40:48] = v[0:8]


def unpack(slot, o, rec, field):
    for i in range(4):
        put(field, 4 * slot + i, o, rec[o, slot, i].astype(f32))


def scaled(plane):
    return (plane.astype(f32) + DIAGONAL) * SCALE


def advance(k, o, segments, levels, pot, circulant, sendf):
    src, prev = levels[k - 1], levels[k - 2]
    for first, planes in segments:
        window = [src[first - 2 + j, o, 8:40] for j in range(planes + 4)]
        v = jnp.concatenate(window[2:-2], axis=0)
        high = v.astype(bf16)
        low = (v - high.astype(f32)).astype(bf16)
        z = jnp.dot(jnp.concatenate([high, low], axis=1), circulant[...], preferred_element_type=f32)
        for i in range(planes):
            p = first + i
            s1 = window[i + 1] + window[i + 3]
            s2 = window[i] + window[i + 4]
            s1 = s1 + (src[p, o, 7:39] + src[p, o, 9:41])
            s2 = s2 + (src[p, o, 6:38] + src[p, o, 10:42])
            w = pot[p] * window[i + 2] + (s1 + z[32 * i : 32 * i + 32] + s2 * SECOND) * FIRST
            w = w * 0.5 if k == 1 else w - prev[p, o, 8:40]
            if k < 6:
                put(levels[k], p, o, w)
            else:
                w = w.astype(bf16)
                sendf[2 * (p - 12), o] = w[0:16]
                sendf[2 * (p - 12) + 1, o] = w[16:32]


def inverse_factor(m):
    n, nb = 128, 16
    row = lax.broadcasted_iota(jnp.int32, (nb, n), 0)
    lane = lax.broadcasted_iota(jnp.int32, (nb, n), 1)
    out = []
    for k in range(n // nb):
        at, lo = k * nb, (k + 1) * nb
        x = m[at:lo]
        cols = [jnp.broadcast_to(x[:, at + t : at + t + 1], (nb, n)) for t in range(nb)]
        own = (lane >= at) & (lane < lo)
        x = jnp.where(own, jnp.where(lane - at == row, 1.0, 0.0), x)
        w = jnp.zeros_like(x)
        for t in range(nb):
            here = row == t
            pivot = jnp.broadcast_to(cols[t][t : t + 1], (nb, n))
            inv = 1.0 / pivot
            r = jnp.broadcast_to(x[t : t + 1], (nb, n))
            w = jnp.where(here, r * lax.rsqrt(pivot), w)
            mult = jnp.where(here, 1.0 - inv, cols[t] * inv)
            x = x - mult * r
            for u in range(t + 1, nb):
                cols[u] = cols[u] - mult * jnp.broadcast_to(cols[u][t : t + 1], (nb, n))
        out.append(jnp.where(lane < lo, w, 0.0))
        if lo < n:
            below = m[lo:]
            lane_b = lax.broadcasted_iota(jnp.int32, below.shape, 1)
            padded = [jnp.zeros((at, n), f32)] * (at > 0) + [x, jnp.zeros((n - lo, n), f32)]
            change = jnp.dot(
                below, jnp.concatenate(padded, 0), precision=lax.Precision.HIGHEST, preferred_element_type=f32
            )
            kept = jnp.where((lane_b >= at) & (lane_b < lo), 0.0, below)
            m = jnp.concatenate([m[:lo], kept - change], axis=0)
    return out


def kernel(
    orb_hbm, pot_hbm, out_hbm,
    orb, potv, potb, potp, poth, potg, poti, send, rec, pot, circulant, sendf, gath,
    part, r1, q1, r2, q2, gram_ref, t_ref, rot, sendr, *rest
):
    levels, (lsem, psem, ssem, rsem, fsem, dsem, gsem, asem, bsem, csem, osem, ready) = rest[:6], rest[6:]
    b, d = lax.axis_index("band"), lax.axis_index("dom")
    yc, zh = d % 8, d // 8
    x, lower = b // 2, b % 2
    me = yc * 8 + b
    above, below = (zh + 1) % 4 * 8, (zh + 3) % 4 * 8

    loadp = pltpu.make_async_copy(pot_hbm, potv, lsem.at[1])
    loadp.start()
    load = pltpu.make_async_copy(orb_hbm, orb, lsem.at[0])
    load.start()

    barrier = pltpu.get_barrier_semaphore()

    def greet(device):
        pl.semaphore_signal(barrier, inc=1, device_id=device, device_id_type=MESH)

    for i in range(1, 8):
        greet((b, zh * 8 + (yc + i) % 8))

    @pl.loop(0, 8)
    def _(k):
        greet((b, above + k))
        greet((b, below + k))

    for i in range(1, 8):
        greet(((b + i) % 8, d))
    greet((b, (zh + 2) % 4 * 8 + yc))
    for i in range(1, 4):
        greet((x * 2 + 1 - lower, (zh + i) % 4 * 8 + yc))

    r = lax.broadcasted_iota(jnp.int32, (128, 128), 0)
    c = lax.broadcasted_iota(jnp.int32, (128, 128), 1)
    apart = (r - c + 128) % 128
    near = jnp.where((apart == 1) | (apart == 127), 1.0, 0.0)
    far = jnp.where((apart == 2) | (apart == 126), SECOND, 0.0)
    for h in range(2):
        circulant[h * 128 : (h + 1) * 128] = (near + far).astype(bf16)

    loadp.wait()
    potb[...] = potv[...].astype(bf16)
    potp[yc] = potb[x]
    pl.semaphore_wait(barrier, 34)

    @pl.when(yc < 3)
    def _():
        for k in range(8):
            remote(potb.at[x], poth.at[3 + yc], psem.at[2], psem.at[3], (b, below + k)).start()

    @pl.when(yc >= 5)
    def _():
        for k in range(8):
            remote(potb.at[x], poth.at[yc - 5], psem.at[2], psem.at[3], (b, above + k)).start()

    for i in range(1, 8):
        remote(potb.at[x], potp.at[yc], psem.at[0], psem.at[1], (b, zh * 8 + (yc + i) % 8)).start()

    load.wait()

    def out_copy(k, o):
        return remote(send.at[o, k], rec.at[o, 3 + yc], ssem.at[o, k], rsem.at[o, 3 + yc], (b, zh * 8 + k))

    def in_copy(k, o):
        return remote(send.at[o, k], rec.at[o, 3 + k], ssem.at[o, 0], rsem.at[o, 3 + k], (b, zh * 8 + k))

    def down(k, o):
        return remote(rec.at[o, 3 + k], rec.at[o, 11 + k], fsem.at[o, k], rsem.at[o, 11 + k], (b, below + yc))

    def up(k, o):
        return remote(rec.at[o, 3 + k], rec.at[o, k - 5], fsem.at[o, k], rsem.at[o, k - 5], (b, above + yc))

    sibling = yc + 1 - 2 * (yc % 2)

    def straight_down(k, o, i):
        return remote(send.at[o, k], rec.at[o, 11 + yc], dsem.at[o, i], rsem.at[o, 11 + yc], (b, below + k))

    def straight_up(k, o, i):
        return remote(send.at[o, k], rec.at[o, yc - 5], dsem.at[o, i], rsem.at[o, yc - 5], (b, above + k))

    def along_x(i, src, dst, sem):
        return remote(src, dst, psem.at[sem], psem.at[sem + 1], ((x + i) % 4 * 2 + lower, d))

    for o in range(2):

        for k in (yc, sibling):
            for j in range(4):
                send[o, k, j] = orb[2 * k + o, j].astype(bf16)

        @pl.when(yc < 3)
        def _():
            straight_down(yc, o, 0).start()
            straight_down(sibling, o, 1).start()

        @pl.when(yc >= 5)
        def _():
            straight_up(yc, o, 0).start()
            straight_up(sibling, o, 1).start()

        @pl.loop(1, 8)
        def _(i):
            k = (yc + i) % 8

            @pl.when(k != sibling)
            def _():
                for j in range(4):
                    send[o, k, j] = orb[2 * k + o, j].astype(bf16)

            out_copy(k, o).start()

        rec[o, 3 + yc] = send[o, yc]

        if o == 0:
            for i in range(1, 8):
                pl.semaphore_signal(ready, inc=1, device_id=((b + i) % 8, d), device_id_type=MESH)
            for i in range(1, 8):
                wait_bytes(send.at[0, 0], ssem.at[0, (yc + i) % 8])

    wait_bytes(potp.at[0:7], psem.at[1])
    for i in range(1, 4):
        along_x(i, potp, potg.at[x], 4).start()
    potg[x] = potp[...]
    wait_bytes(poth, psem.at[3])
    for i in range(1, 4):
        along_x(i, poth, poti.at[x], 6).start()
    poti[x] = poth[...]

    def forward(k, o):
        @pl.when(yc // 2 != k // 2)
        def _():
            (down if k < 3 else up)(k, o).start()

    def receive(o, to_forward):
        for k in (0, 7, 1, 6, 2, 5, 3, 4):

            @pl.when(yc != k)
            def _():
                in_copy(k, o).wait_recv()

            if k in to_forward:
                forward(k, o)
            unpack(3 + k, o, rec, levels[0])

    step = functools.partial(advance, levels=levels, pot=pot, circulant=circulant, sendf=sendf)

    def inner(o):
        for k in range(1, 7):
            step(k, o, [(12 + 2 * k, 32 - 4 * k)])

    own = b * 16 + yc * 2

    def deliver(to, orbitals=(0, 1)):
        @pl.loop(0, 8)
        def _(i):
            band = (b + 4 + i) % 8
            q = to * 8 + band
            part_of = pl.ds(orbitals[0], len(orbitals))

            @pl.when(q != me)
            def _():
                remote(
                    sendf.at[q, part_of],
                    gath.at[pl.ds(own + orbitals[0], len(orbitals))],
                    gsem.at[0],
                    gsem.at[1],
                    (band, zh * 8 + to),
                ).start()

    def halo(s, o):
        up(7 - s, o).wait_recv()
        down(s, o).wait_recv()
        unpack(2 - s, o, rec, levels[0])
        unpack(11 + s, o, rec, levels[0])

    def piece(s):
        for k in range(1, 7):
            step(k, 1, [(8 - 4 * s + 2 * k, 4), (44 + 4 * s - 2 * k, 4)])

    receive(0, (0, 7, 1, 6, 2, 5))
    receive(1, (0, 7, 1, 6))
    wait_bytes(potg.at[0:3], psem.at[5])

    @pl.loop(0, 8)
    def _(s):
        for i in range(4):
            pot[12 + 4 * s + i] = scaled(potg[i, s])

    inner(0)
    forward(2, 1)
    forward(5, 1)
    inner(1)
    pl.semaphore_wait(ready, 7)
    deliver(3)
    deliver(4)

    wait_bytes(poti.at[0:3], psem.at[7])
    for s in range(3):
        for i in range(4):
            pot[4 * s + i] = scaled(poti[i, s])
            pot[44 + 4 * s + i] = scaled(poti[i, 3 + s])

    for s in range(3):
        halo(s, 0)
    for k in range(1, 7):
        step(k, 0, [(2 * k, 12), (44 - 2 * k, 12)])
    deliver(0, (0,))
    deliver(7, (0,))

    for s in range(2):
        halo(s, 1)
    for k in range(1, 7):
        step(k, 1, [(4 + 2 * k, 8), (44 - 2 * k, 8)])
    for s in range(2):
        deliver(2 - s)
        deliver(5 + s)

    halo(2, 1)
    piece(2)
    deliver(0, (1,))
    deliver(7, (1,))

    gath[pl.ds(own, 2)] = sendf[me]

    wait_bytes(potp.at[0:7], psem.at[0])

    @pl.when((yc < 3) | (yc >= 5))
    def _():
        wait_bytes(potp, psem.at[2])

    wait_bytes(potg.at[0:3], psem.at[4])
    wait_bytes(poti.at[0:3], psem.at[6])
    for o in range(2):
        for i in range(1, 8):
            if o == 1:
                out_copy((yc + i) % 8, o).wait_send()
        for k in (0, 1, 2, 5, 6, 7):

            @pl.when(yc // 2 != k // 2)
            def _():
                wait_bytes(send.at[0, 0], fsem.at[o, k])

        @pl.when((yc < 3) | (yc >= 5))
        def _():
            for i in range(2):
                wait_bytes(send.at[0, 0], dsem.at[o, i])

    wait_bytes(gath.at[0:126], gsem.at[1])

    t = jnp.swapaxes(gath[...].astype(f32), 0, 1).astype(bf16)
    t_ref[...] = t
    cells = jnp.concatenate([t[j] for j in range(16)], axis=1)
    gram = lax.dot_general(cells, cells, (((1,), (1,)), ((), ())), preferred_element_type=f32)
    part[...] = gram.reshape(32, 4, 128)
    mine, level = x * 8 + yc, zh * 2 + lower

    def others(send_to):
        for i in range(32):
            if i != 20:
                col, row = (x + (i // 8 + 2) % 4) % 4, (yc + (i + 4) % 8) % 8
                send_to(col * 8 + row, (col * 2 + lower, zh * 8 + row))

    @others
    def _(j, device):
        remote(part.at[j], r1.at[mine], asem.at[0], asem.at[1], device).start()

    r1[mine] = part[mine]
    wait_bytes(r1.at[0:31], asem.at[1])
    q1[...] = jnp.sum(r1[...], axis=0)
    for i in (4, 3, 5, 2, 6, 1, 7):
        j = (level + i) % 8
        remote(q1, r2.at[level], asem.at[2], asem.at[3], (x * 2 + j % 2, j // 2 * 8 + yc)).start()
    r2[level] = q1[...]
    wait_bytes(r2.at[0:7], asem.at[3])
    q2[...] = jnp.sum(r2[...], axis=0)

    @others
    def _(j, device):
        remote(q2, gram_ref.at[mine], asem.at[4], asem.at[5], device).start()

    gram_ref[mine] = q2[...]
    wait_bytes(gram_ref.at[0:31], asem.at[5])
    inverse = inverse_factor(gram_ref[...].reshape(128, 128) * (1.0 / 2.0**19))
    w = jnp.concatenate([block.astype(bf16) for block in inverse], axis=0)
    for j in range(16):
        rot[j] = jnp.dot(w, t_ref[j], preferred_element_type=f32)

    def turned(k):
        return jnp.swapaxes(rot[:, pl.ds(pl.multiple_of(16 * k, 16), 16), :], 0, 1).astype(bf16)

    def cells_of(band):
        return out_hbm.at[:, band // 2, pl.ds(pl.multiple_of(band % 2 * 16, 16), 16), :]

    def back_copy(i):
        k = (b + i) % 8
        return remote(sendr.at[k], cells_of(b), bsem.at[i], csem.at[b], (k, d))

    @pl.loop(1, 8)
    def _(i):
        k = (b + i) % 8
        sendr[k] = turned(k)
        back_copy(i).start()

    sendr[b] = turned(b)
    stay = pltpu.make_async_copy(sendr.at[b], cells_of(b), osem.at[0])
    stay.start()

    wait_bytes(gath.at[0:126], gsem.at[0])
    wait_bytes(r1.at[0:31], asem.at[0])
    wait_bytes(r2.at[0:7], asem.at[2])
    wait_bytes(r1.at[0:31], asem.at[4])
    for i in range(1, 8):
        back_copy(i).wait_send()
    for i in range(1, 8):
        k = (b + 8 - i) % 8
        remote(sendr.at[k], cells_of(k), bsem.at[0], csem.at[k], (k, d)).wait_recv()
    stay.wait()


def body(orbitals, potential):
    dma = pltpu.SemaphoreType.DMA
    rotated = pl.pallas_call(
        kernel,
        out_shape=jax.ShapeDtypeStruct((16, 4, 32, 128), bf16),
        in_specs=[ANY, ANY],
        out_specs=VMEM,
        scratch_shapes=[
            pltpu.VMEM((16, 4, 32, 128), f32),
            pltpu.VMEM((4, 32, 128), f32),
            pltpu.VMEM((4, 32, 128), bf16),
            pltpu.VMEM((8, 32, 128), bf16),
            pltpu.VMEM((6, 32, 128), bf16),
            pltpu.VMEM((4, 8, 32, 128), bf16),
            pltpu.VMEM((4, 6, 32, 128), bf16),
            pltpu.VMEM((2, 8, 4, 32, 128), bf16),
            pltpu.VMEM((2, 14, 4, 32, 128), bf16),
            pltpu.VMEM((56, 32, 128), f32),
            pltpu.VMEM((256, 128), bf16),
            pltpu.VMEM((64, 2, 16, 128), bf16),
            pltpu.VMEM((128, 16, 128), bf16),
            pltpu.VMEM((32, 4, 128), f32),
            pltpu.VMEM((32, 4, 128), f32),
            pltpu.VMEM((4, 128), f32),
            pltpu.VMEM((8, 4, 128), f32),
            pltpu.VMEM((4, 128), f32),
            pltpu.VMEM((32, 4, 128), f32),
            pltpu.VMEM((16, 128, 128), bf16),
            pltpu.VMEM((16, 128, 128), f32),
            pltpu.VMEM((8, 16, 16, 128), bf16),
        ]
        + [pltpu.VMEM((56, 2, 48, 128), f32)] * 6
        + [dma((2,)), dma((8,)), dma((2, 8)), dma((2, 14)), dma((2, 8)), dma((2, 2)), dma((2,)), dma((8,)), dma((8,)), dma((8,)), dma((8,)), pltpu.SemaphoreType.REGULAR],
        compiler_params=pltpu.CompilerParams(collective_id=0, has_side_effects=True, vmem_limit_bytes=54400 << 10),
    )(orbitals, potential)
    return rotated.astype(f32)


def solution(mesh):
    placed = (P("band", "dom", None, None), P("dom", None, None))
    return jax.shard_map(
        body, mesh=mesh, in_specs=placed, out_specs=P("band", "dom", None, None), check_vma=False
    )
```

```python
import functools

import jax
import jax.numpy as jnp
from jax import lax
from jax.experimental import pallas as pl
from jax.experimental.pallas import tpu as pltpu
from jax.sharding import PartitionSpec as P

MESH = pl.DeviceIdType.MESH
f32, bf16 = jnp.float32, jnp.bfloat16

centre = 5.5
half = 4.5
SCALE = 2.0 / half
DIAGONAL = 0.5 * 7.5 - centre
FIRST = -0.5 * (4.0 / 3.0) * SCALE
SECOND = -1.0 / 16.0

VMEM = pl.BlockSpec(memory_space=pltpu.VMEM)
ANY = pl.BlockSpec(memory_space=pl.ANY)


def remote(src, dst, send_sem, recv_sem, device):
    return pltpu.make_async_remote_copy(
        src_ref=src, dst_ref=dst, send_sem=send_sem, recv_sem=recv_sem, device_id=device, device_id_type=MESH
    )


def wait_bytes(ref, sem):
    pltpu.make_async_copy(ref, ref, sem).wait()


def put(dst, p, o, v):
    dst[p, o, 8:40] = v
    dst[p, o, 0:8] = v[24:32]
    dst[p, o, 40:48] = v[0:8]


def unpack(slot, o, rec, field):
    for i in range(4):
        put(field, 4 * slot + i, o, rec[o, slot, i].astype(f32))


def scaled(plane):
    return (plane.astype(f32) + DIAGONAL) * SCALE


def advance(k, o, segments, levels, pot, circulant, sendf):
    src, prev = levels[k - 1], levels[k - 2]
    for first, planes in segments:
        window = [src[first - 2 + j, o, 8:40] for j in range(planes + 4)]
        v = jnp.concatenate(window[2:-2], axis=0)
        high = v.astype(bf16)
        low = (v - high.astype(f32)).astype(bf16)
        z = jnp.dot(jnp.concatenate([high, low], axis=1), circulant[...], preferred_element_type=f32)
        for i in range(planes):
            p = first + i
            s1 = window[i + 1] + window[i + 3]
            s2 = window[i] + window[i + 4]
            s1 = s1 + (src[p, o, 7:39] + src[p, o, 9:41])
            s2 = s2 + (src[p, o, 6:38] + src[p, o, 10:42])
            w = (s1 + z[32 * i : 32 * i + 32] + s2 * SECOND) * FIRST
            if pot is None:
                levels[k][p, o, 8:40] = w
                continue
            w = pot[p] * window[i + 2] + w
            w = w * 0.5 if k == 1 else w - prev[p, o, 8:40]
            if k < 6:
                put(levels[k], p, o, w)
            else:
                w = w.astype(bf16)
                sendf[2 * (p - 12), o] = w[0:16]
                sendf[2 * (p - 12) + 1, o] = w[16:32]


def inverse_factor(m):
    n, nb = 128, 16
    row = lax.broadcasted_iota(jnp.int32, (nb, n), 0)
    lane = lax.broadcasted_iota(jnp.int32, (nb, n), 1)
    out = []
    for k in range(n // nb):
        at, lo = k * nb, (k + 1) * nb
        x = m[at:lo]
        cols = [jnp.broadcast_to(x[:, at + t : at + t + 1], (nb, n)) for t in range(nb)]
        own = (lane >= at) & (lane < lo)
        x = jnp.where(own, jnp.where(lane - at == row, 1.0, 0.0), x)
        w = jnp.zeros_like(x)
        for t in range(nb):
            here = row == t
            pivot = jnp.broadcast_to(cols[t][t : t + 1], (nb, n))
            inv = 1.0 / pivot
            r = jnp.broadcast_to(x[t : t + 1], (nb, n))
            w = jnp.where(here, r * lax.rsqrt(pivot), w)
            mult = jnp.where(here, 1.0 - inv, cols[t] * inv)
            x = x - mult * r
            for u in range(t + 1, nb):
                cols[u] = cols[u] - mult * jnp.broadcast_to(cols[u][t : t + 1], (nb, n))
        out.append(jnp.where(lane < lo, w, 0.0))
        if lo < n:
            below = m[lo:]
            lane_b = lax.broadcasted_iota(jnp.int32, below.shape, 1)
            padded = [jnp.zeros((at, n), f32)] * (at > 0) + [x, jnp.zeros((n - lo, n), f32)]
            change = jnp.dot(
                below, jnp.concatenate(padded, 0), precision=lax.Precision.HIGHEST, preferred_element_type=f32
            )
            kept = jnp.where((lane_b >= at) & (lane_b < lo), 0.0, below)
            m = jnp.concatenate([m[:lo], kept - change], axis=0)
    return out


def kernel(
    orb_hbm, pot_hbm, out_hbm,
    orb, potv, potb, potp, poth, potg, poti, send, rec, pot, circulant, sendf, gath,
    part, r1, q1, r2, q2, gram_ref, t_ref, rot, sendr, *rest
):
    levels, (lsem, psem, ssem, rsem, fsem, dsem, gsem, asem, bsem, csem, osem, ready) = rest[:6], rest[6:]
    b, d = lax.axis_index("band"), lax.axis_index("dom")
    yc, zh = d % 8, d // 8
    x, lower = b // 2, b % 2
    me = yc * 8 + b
    above, below = (zh + 1) % 4 * 8, (zh + 3) % 4 * 8

    loadp = pltpu.make_async_copy(pot_hbm, potv, lsem.at[1])
    loadp.start()
    load = pltpu.make_async_copy(orb_hbm, orb, lsem.at[0])
    load.start()

    barrier = pltpu.get_barrier_semaphore()

    def greet(device):
        pl.semaphore_signal(barrier, inc=1, device_id=device, device_id_type=MESH)

    for i in range(1, 8):
        greet((b, zh * 8 + (yc + i) % 8))

    @pl.loop(0, 8)
    def _(k):
        greet((b, above + k))
        greet((b, below + k))

    for i in range(1, 8):
        greet(((b + i) % 8, d))
    greet((b, (zh + 2) % 4 * 8 + yc))
    for i in range(1, 4):
        greet((x * 2 + 1 - lower, (zh + i) % 4 * 8 + yc))

    r = lax.broadcasted_iota(jnp.int32, (128, 128), 0)
    c = lax.broadcasted_iota(jnp.int32, (128, 128), 1)
    apart = (r - c + 128) % 128
    near = jnp.where((apart == 1) | (apart == 127), 1.0, 0.0)
    far = jnp.where((apart == 2) | (apart == 126), SECOND, 0.0)
    for h in range(2):
        circulant[h * 128 : (h + 1) * 128] = (near + far).astype(bf16)

    loadp.wait()
    potb[...] = potv[...].astype(bf16)
    potp[yc] = potb[x]
    pl.semaphore_wait(barrier, 34)

    @pl.when(yc < 3)
    def _():
        for k in range(8):
            remote(potb.at[x], poth.at[3 + yc], psem.at[2], psem.at[3], (b, below + k)).start()

    @pl.when(yc >= 5)
    def _():
        for k in range(8):
            remote(potb.at[x], poth.at[yc - 5], psem.at[2], psem.at[3], (b, above + k)).start()

    for i in (4, 3, 5, 2, 6, 1, 7):
        remote(potb.at[x], potp.at[yc], psem.at[0], psem.at[1], (b, zh * 8 + (yc + i) % 8)).start()

    load.wait()

    def out_copy(k, o):
        return remote(send.at[o, k], rec.at[o, 3 + yc], ssem.at[o, k], rsem.at[o, 3 + yc], (b, zh * 8 + k))

    def in_copy(k, o):
        return remote(send.at[o, k], rec.at[o, 3 + k], ssem.at[o, 0], rsem.at[o, 3 + k], (b, zh * 8 + k))

    def down(k, o):
        return remote(rec.at[o, 3 + k], rec.at[o, 11 + k], fsem.at[o, k], rsem.at[o, 11 + k], (b, below + yc))

    def up(k, o):
        return remote(rec.at[o, 3 + k], rec.at[o, k - 5], fsem.at[o, k], rsem.at[o, k - 5], (b, above + yc))

    sibling = yc + 1 - 2 * (yc % 2)

    def straight_down(k, o, i):
        return remote(send.at[o, k], rec.at[o, 11 + yc], dsem.at[o, i], rsem.at[o, 11 + yc], (b, below + k))

    def straight_up(k, o, i):
        return remote(send.at[o, k], rec.at[o, yc - 5], dsem.at[o, i], rsem.at[o, yc - 5], (b, above + k))

    def along_x(i, src, dst, sem):
        return remote(src, dst, psem.at[sem], psem.at[sem + 1], ((x + i) % 4 * 2 + lower, d))

    for o in range(2):

        for k in (yc, sibling):
            for j in range(4):
                send[o, k, j] = orb[2 * k + o, j].astype(bf16)

        @pl.when(yc < 3)
        def _():
            straight_down(yc, o, 0).start()
            straight_down(sibling, o, 1).start()

        @pl.when(yc >= 5)
        def _():
            straight_up(yc, o, 0).start()
            straight_up(sibling, o, 1).start()

        @pl.loop(1, 8)
        def _(i):
            k = (yc + i) % 8

            @pl.when(k != sibling)
            def _():
                for j in range(4):
                    send[o, k, j] = orb[2 * k + o, j].astype(bf16)

            out_copy(k, o).start()

        rec[o, 3 + yc] = send[o, yc]

        if o == 0:
            for i in range(1, 8):
                pl.semaphore_signal(ready, inc=1, device_id=((b + i) % 8, d), device_id_type=MESH)
            for i in range(1, 8):
                wait_bytes(send.at[0, 0], ssem.at[0, (yc + i) % 8])

    wait_bytes(potp.at[0:7], psem.at[1])
    for i in (2, 1, 3):
        along_x(i, potp, potg.at[x], 4).start()
    potg[x] = potp[...]
    wait_bytes(poth, psem.at[3])
    for i in (2, 1, 3):
        along_x(i, poth, poti.at[x], 6).start()
    poti[x] = poth[...]

    def forward(k, o):
        @pl.when(yc // 2 != k // 2)
        def _():
            (down if k < 3 else up)(k, o).start()

    def receive(o, to_forward):
        for k in (0, 7, 1, 6, 2, 5, 3, 4):

            @pl.when(yc != k)
            def _():
                in_copy(k, o).wait_recv()

            if k in to_forward:
                forward(k, o)
            unpack(3 + k, o, rec, levels[0])

    step = functools.partial(advance, levels=levels, pot=pot, circulant=circulant, sendf=sendf)

    def inner(o):
        for p in range(14, 42):
            w = (pot[p] * levels[0][p, o, 8:40] + levels[1][p, o, 8:40]) * 0.5
            put(levels[1], p, o, w)
        for k in range(2, 7):
            step(k, o, [(12 + 2 * k, 32 - 4 * k)])

    own = b * 16 + yc * 2

    def deliver(to, orbitals=(0, 1)):
        @pl.loop(0, 8)
        def _(i):
            band = (b + 4 + i) % 8
            q = to * 8 + band
            part_of = pl.ds(orbitals[0], len(orbitals))

            @pl.when(q != me)
            def _():
                remote(
                    sendf.at[q, part_of],
                    gath.at[pl.ds(own + orbitals[0], len(orbitals))],
                    gsem.at[0],
                    gsem.at[1],
                    (band, zh * 8 + to),
                ).start()

    def halo(s, o):
        up(7 - s, o).wait_recv()
        down(s, o).wait_recv()
        unpack(2 - s, o, rec, levels[0])
        unpack(11 + s, o, rec, levels[0])

    def piece(s):
        for k in range(1, 7):
            step(k, 1, [(8 - 4 * s + 2 * k, 4), (44 + 4 * s - 2 * k, 4)])

    receive(0, (0, 7, 1, 6, 2, 5))
    receive(1, (0, 7, 1, 6))
    for o in range(2):
        advance(1, o, [(14, 28)], levels, None, circulant, sendf)
    wait_bytes(potg.at[0:3], psem.at[5])

    @pl.loop(0, 8)
    def _(s):
        for i in range(4):
            pot[12 + 4 * s + i] = scaled(potg[i, s])

    inner(0)
    forward(2, 1)
    forward(5, 1)
    inner(1)
    pl.semaphore_wait(ready, 7)
    deliver(3)
    deliver(4)

    wait_bytes(poti.at[0:3], psem.at[7])
    for s in range(3):
        for i in range(4):
            pot[4 * s + i] = scaled(poti[i, s])
            pot[44 + 4 * s + i] = scaled(poti[i, 3 + s])

    for s in range(3):
        halo(s, 0)
    for k in range(1, 7):
        step(k, 0, [(2 * k, 12), (44 - 2 * k, 12)])
    deliver(0, (0,))
    deliver(7, (0,))

    for s in range(2):
        halo(s, 1)
    for k in range(1, 7):
        step(k, 1, [(4 + 2 * k, 8), (44 - 2 * k, 8)])
    for s in range(2):
        deliver(2 - s)
        deliver(5 + s)

    halo(2, 1)
    piece(2)
    deliver(0, (1,))
    deliver(7, (1,))

    gath[pl.ds(own, 2)] = sendf[me]

    wait_bytes(potp.at[0:7], psem.at[0])

    @pl.when((yc < 3) | (yc >= 5))
    def _():
        wait_bytes(potp, psem.at[2])

    wait_bytes(potg.at[0:3], psem.at[4])
    wait_bytes(poti.at[0:3], psem.at[6])
    for o in range(2):
        for i in range(1, 8):
            if o == 1:
                out_copy((yc + i) % 8, o).wait_send()
        for k in (0, 1, 2, 5, 6, 7):

            @pl.when(yc // 2 != k // 2)
            def _():
                wait_bytes(send.at[0, 0], fsem.at[o, k])

        @pl.when((yc < 3) | (yc >= 5))
        def _():
            for i in range(2):
                wait_bytes(send.at[0, 0], dsem.at[o, i])

    wait_bytes(gath.at[0:126], gsem.at[1])

    t = jnp.swapaxes(gath[...].astype(f32), 0, 1).astype(bf16)
    t_ref[...] = t
    cells = jnp.concatenate([t[j] for j in range(16)], axis=1)
    gram = lax.dot_general(cells, cells, (((1,), (1,)), ((), ())), preferred_element_type=f32)
    part[...] = gram.reshape(32, 4, 128)
    mine, level = x * 8 + yc, zh * 2 + lower

    def others(send_to):
        for i in range(32):
            if i != 20:
                col, row = (x + (i // 8 + 2) % 4) % 4, (yc + (i + 4) % 8) % 8
                send_to(col * 8 + row, (col * 2 + lower, zh * 8 + row))

    @others
    def _(j, device):
        remote(part.at[j], r1.at[mine], asem.at[0], asem.at[1], device).start()

    r1[mine] = part[mine]
    wait_bytes(r1.at[0:31], asem.at[1])
    q1[...] = jnp.sum(r1[...], axis=0)
    for i in (4, 3, 5, 2, 6, 1, 7):
        j = (level + i) % 8
        remote(q1, r2.at[level], asem.at[2], asem.at[3], (x * 2 + j % 2, j // 2 * 8 + yc)).start()
    r2[level] = q1[...]
    wait_bytes(r2.at[0:7], asem.at[3])
    q2[...] = jnp.sum(r2[...], axis=0)

    @others
    def _(j, device):
        remote(q2, gram_ref.at[mine], asem.at[4], asem.at[5], device).start()

    gram_ref[mine] = q2[...]
    wait_bytes(gram_ref.at[0:31], asem.at[5])
    inverse = inverse_factor(gram_ref[...].reshape(128, 128) * (1.0 / 2.0**19))
    w = jnp.concatenate([block.astype(bf16) for block in inverse], axis=0)
    for j in range(16):
        rot[j] = jnp.dot(w, t_ref[j], preferred_element_type=f32)

    def turned(k):
        return jnp.swapaxes(rot[:, pl.ds(pl.multiple_of(16 * k, 16), 16), :], 0, 1).astype(bf16)

    def cells_of(band):
        return out_hbm.at[:, band // 2, pl.ds(pl.multiple_of(band % 2 * 16, 16), 16), :]

    def back_copy(i):
        k = (b + i) % 8
        return remote(sendr.at[k], cells_of(b), bsem.at[i], csem.at[b], (k, d))

    @pl.loop(1, 8)
    def _(i):
        k = (b + i) % 8
        sendr[k] = turned(k)
        back_copy(i).start()

    sendr[b] = turned(b)
    stay = pltpu.make_async_copy(sendr.at[b], cells_of(b), osem.at[0])
    stay.start()

    wait_bytes(gath.at[0:126], gsem.at[0])
    wait_bytes(r1.at[0:31], asem.at[0])
    wait_bytes(r2.at[0:7], asem.at[2])
    wait_bytes(r1.at[0:31], asem.at[4])
    for i in range(1, 8):
        back_copy(i).wait_send()
    for i in range(1, 8):
        k = (b + 8 - i) % 8
        remote(sendr.at[k], cells_of(k), bsem.at[0], csem.at[k], (k, d)).wait_recv()
    stay.wait()


def body(orbitals, potential):
    dma = pltpu.SemaphoreType.DMA
    rotated = pl.pallas_call(
        kernel,
        out_shape=jax.ShapeDtypeStruct((16, 4, 32, 128), bf16),
        in_specs=[ANY, ANY],
        out_specs=VMEM,
        scratch_shapes=[
            pltpu.VMEM((16, 4, 32, 128), f32),
            pltpu.VMEM((4, 32, 128), f32),
            pltpu.VMEM((4, 32, 128), bf16),
            pltpu.VMEM((8, 32, 128), bf16),
            pltpu.VMEM((6, 32, 128), bf16),
            pltpu.VMEM((4, 8, 32, 128), bf16),
            pltpu.VMEM((4, 6, 32, 128), bf16),
            pltpu.VMEM((2, 8, 4, 32, 128), bf16),
            pltpu.VMEM((2, 14, 4, 32, 128), bf16),
            pltpu.VMEM((56, 32, 128), f32),
            pltpu.VMEM((256, 128), bf16),
            pltpu.VMEM((64, 2, 16, 128), bf16),
            pltpu.VMEM((128, 16, 128), bf16),
            pltpu.VMEM((32, 4, 128), f32),
            pltpu.VMEM((32, 4, 128), f32),
            pltpu.VMEM((4, 128), f32),
            pltpu.VMEM((8, 4, 128), f32),
            pltpu.VMEM((4, 128), f32),
            pltpu.VMEM((32, 4, 128), f32),
            pltpu.VMEM((16, 128, 128), bf16),
            pltpu.VMEM((16, 128, 128), f32),
            pltpu.VMEM((8, 16, 16, 128), bf16),
        ]
        + [pltpu.VMEM((56, 2, 48, 128), f32)] * 6
        + [dma((2,)), dma((8,)), dma((2, 8)), dma((2, 14)), dma((2, 8)), dma((2, 2)), dma((2,)), dma((8,)), dma((8,)), dma((8,)), dma((8,)), pltpu.SemaphoreType.REGULAR],
        compiler_params=pltpu.CompilerParams(collective_id=0, has_side_effects=True, vmem_limit_bytes=54400 << 10),
    )(orbitals, potential)
    return rotated.astype(f32)


def solution(mesh):
    placed = (P("band", "dom", None, None), P("dom", None, None))
    return jax.shard_map(
        body, mesh=mesh, in_specs=placed, out_specs=P("band", "dom", None, None), check_vma=False
    )
```
